32 devices in a mesh: dp: 2 (over x), ctx: 4 (over z), exp: 4 (over y, core).
Axes of the slice: x: 2, y: 2, z: 4, core: 2. Of those that a mesh axis runs over, the one named last changes fastest.
Arguments:
- tokens: bfloat16 [8, 1024, 1024], P(('dp', 'exp'), 'ctx'), may hold values from -6 to 6
- qkv_weight: bfloat16 [1024, 3072], P(('dp', 'ctx', 'exp')), may hold values from -0.1875 to 0.1875
- out_weight: bfloat16 [1024, 1024], P(('dp', 'ctx', 'exp')), may hold values from -1 to 1
- norm1_gain: bfloat16 [1024], P(('dp', 'ctx', 'exp')), may hold values from 0.5 to 1.5
- norm1_shift: bfloat16 [1024], P(('dp', 'ctx', 'exp')), may hold values from -1.75 to 1.75
- norm2_gain: bfloat16 [1024], P(('dp', 'ctx', 'exp')), may hold values from 0.5 to 1.5
- norm2_shift: bfloat16 [1024], P(('dp', 'ctx', 'exp')), may hold values from -1.75 to 1.75
- inner_weight: bfloat16 [1024, 4096], P(('dp', 'ctx', 'exp')), may hold values from -0.1875 to 0.1875
- outer_weight: bfloat16 [4096, 1024], P(('dp', 'ctx', 'exp')), may hold values from -0.09375 to 0.09375
- router_weight: bfloat16 [1024, 4], P(('dp', 'ctx', 'exp')), may hold values from -0.09375 to 0.09375
- expert_inner: bfloat16 [4, 1024, 4096], P('exp', None, ('dp', 'ctx')), may hold values from -0.1875 to 0.1875
- expert_outer: bfloat16 [4, 4096, 1024], P('exp', ('dp', 'ctx')), may hold values from -0.375 to 0.375
- segments: int32 [8, 1024], P(('dp', 'exp')), may hold values from 0 to 2, as said below
- routes: int32 [8, 1024, 1], P(('dp', 'exp'), 'ctx'), may hold values from 0 to 3
- priority: int32 [8, 4, 256], P(('dp', 'exp'), 'ctx'), may hold values from 0 to 255, each once within a row
- cotangent: bfloat16 [8, 1024, 1024], P(('dp', 'exp'), 'ctx'), may hold values from -6 to 6
Outputs:
- output: bfloat16 [8, 1024, 1024], P(('dp', 'exp'), 'ctx')
- d_tokens: float32 [8, 1024, 1024], P(('dp', 'exp'), 'ctx')
- d_qkv_weight: float32 [1024, 3072], P(('dp', 'ctx', 'exp'))
- d_out_weight: float32 [1024, 1024], P(('dp', 'ctx', 'exp'))
- d_norm1_gain: float32 [1024], P(('dp', 'ctx', 'exp'))
- d_norm1_shift: float32 [1024], P(('dp', 'ctx', 'exp'))
- d_norm2_gain: float32 [1024], P(('dp', 'ctx', 'exp'))
- d_norm2_shift: float32 [1024], P(('dp', 'ctx', 'exp'))
- d_inner_weight: float32 [1024, 4096], P(('dp', 'ctx', 'exp'))
- d_outer_weight: float32 [4096, 1024], P(('dp', 'ctx', 'exp'))
- d_router_weight: float32 [1024, 4], P(('dp', 'ctx', 'exp'))
- d_expert_inner: float32 [4, 1024, 4096], P('exp', None, ('dp', 'ctx'))
- d_expert_outer: float32 [4, 4096, 1024], P('exp', ('dp', 'ctx'))
The draws below stay inside these ranges and needn't reach their ends.
Inputs may be any that keep to these rules, and one draw needn't show every extreme that they name: `segments`: each sequence packs documents 0, 1 and 2 in order; document 1 starts at a position from 128 to 255 and document 2 at one from 769 to 896. `routes`: every expert is chosen by some token. `priority`: within each block of 256 positions of a sequence every number from 0 to 255 appears once.
All inputs are finite; a program needn't handle non-finite values.
Results may differ from the reference program's by a relative error of at most 0.028.
Values may be sent and summed in bfloat16 or wider, within the bound.
No kernel may reach another device: no remote copies, remote signals or barrier semaphores. Data moves between devices by JAX's collectives and lax.ppermute only.
A program may use at most 256 MiB of HBM per device.

```python
import math
import jax
import jax.numpy as jnp
from jax import lax

D = 1024
HEADS = 16
HEAD_DIM = 64
FF = 4096
EFF = 4096
TOK_DEV = 256
EXPERTS = 4
SEQS = 8
SPLITS = 4
SEQ_LEN = 1024
N_CTX = 4


def draw_segments(key, part):
    first_key = jax.random.fold_in(key, 11)
    second_key = jax.random.fold_in(key, 23)
    starts = jax.random.randint(first_key, (SEQS, 1), TOK_DEV // 2, TOK_DEV)
    finishes = jax.random.randint(second_key, (SEQS, 1), SEQ_LEN - TOK_DEV + 1, SEQ_LEN - TOK_DEV // 2 + 1)
    positions = jnp.arange(SEQ_LEN, dtype=jnp.int32)[None, :]
    return (positions >= starts).astype(jnp.int32) + (positions >= finishes).astype(jnp.int32)


def block_scale(stream_key, shape, cuts, smallest, largest):
    factor_of, own = 1.0, jax.random.fold_in(stream_key, 6)
    for axis_at, parts in cuts:
        heights = jnp.exp(jax.random.uniform(jax.random.fold_in(own, axis_at), (parts,), jnp.float32, smallest / len(cuts), largest / len(cuts)))
        factor_of = factor_of * jnp.repeat(heights, shape[axis_at] // parts).reshape([-1 if axis == axis_at else 1 for axis in range(len(shape))])
    return factor_of


def distinct(stream_key, rows, count, top, lift):
    sequence = jax.random.permutation(jax.random.fold_in(stream_key, 1), count)
    boost = sequence
    for power in range(3):
        boost = boost * boost // count
    boost = boost * lift // count
    chance = jax.random.randint(jax.random.fold_in(stream_key, 2), (rows, count), 0, 4096) + boost
    holders = jax.random.permutation(jax.random.fold_in(stream_key, 3), rows)[jnp.arange(count) % rows]
    chance = jnp.where(jnp.arange(rows)[:, None] == holders[None, :], 1 << 14, chance)
    merit = chance * count + jnp.arange(count)
    return lax.top_k(merit.astype(jnp.int32), top)[1].astype(jnp.int32)


def bell_draw(rng, dims, scale, bound, cuts=(), kind=jnp.bfloat16):
    array = jax.random.normal(rng, dims, jnp.float32) * scale
    if len(cuts) > 0:
        array = block_scale(rng, dims, cuts, -0.22, 0.18) * array
    return jnp.clip(array, min=-bound, max=bound).astype(kind)


def setup_inputs(seed: int = 0) -> dict:
    keys = jax.random.split(jax.random.key(seed), 17)
    tokens = bell_draw(keys[0], (SEQS, SEQ_LEN, D), 1.0, 6.0, ((0, 8), (1, 4)))
    qkv_weight = bell_draw(keys[1], (D, 3 * D), D ** -0.5, 0.1875, ((0, 32),))
    out_weight = bell_draw(keys[2], (D, D), (D // 32) ** -0.5, 1.0, ((0, 32),))
    norm1_gain = jnp.clip(1.0 + 0.1 * jax.random.normal(keys[3], (D,), jnp.float32), 0.5, 1.5).astype(jnp.bfloat16)
    norm1_shift = bell_draw(keys[4], (D,), 0.3, 1.75, ((0, 32),))
    norm2_gain = jnp.clip(1.0 + 0.1 * jax.random.normal(keys[5], (D,), jnp.float32), 0.5, 1.5).astype(jnp.bfloat16)
    norm2_shift = bell_draw(keys[6], (D,), 0.3, 1.75, ((0, 32),))
    inner_weight = bell_draw(keys[7], (D, FF), D ** -0.5, 0.1875, ((0, 32),))
    outer_weight = bell_draw(keys[8], (FF, D), FF ** -0.5, 0.09375, ((0, 32),))
    router_weight = bell_draw(keys[9], (D, EXPERTS), (4 * D) ** -0.5, 0.09375, ((0, 32),))
    expert_inner = bell_draw(keys[10], (EXPERTS, D, EFF), D ** -0.5, 0.1875, ((0, 4), (2, 8)))
    expert_outer = bell_draw(keys[11], (EXPERTS, EFF, D), (max(1, EFF // (EXPERTS * EXPERTS))) ** -0.5, 0.375, ((0, 4), (1, 8)))
    segments = draw_segments(jax.random.fold_in(keys[16], 71), 0)
    routes = distinct(keys[13], SEQS * SEQ_LEN, EXPERTS, 1, 2048).reshape((SEQS, SEQ_LEN, 1))
    priority = jax.vmap(lambda own: jax.random.permutation(own, TOK_DEV))(jax.random.split(keys[14], SEQS * SPLITS)).reshape((SEQS, SPLITS, TOK_DEV)).astype(jnp.int32)
    cotangent = bell_draw(keys[15], (SEQS, SEQ_LEN, D), 1.0, 6.0, ((0, 8), (1, 4)))
    return dict(tokens=tokens, qkv_weight=qkv_weight, out_weight=out_weight, norm1_gain=norm1_gain, norm1_shift=norm1_shift, norm2_gain=norm2_gain, norm2_shift=norm2_shift, inner_weight=inner_weight, outer_weight=outer_weight, router_weight=router_weight, expert_inner=expert_inner, expert_outer=expert_outer, segments=segments, routes=routes, priority=priority, cotangent=cotangent)


@jax.custom_vjp
def low(v):
    return lax.optimization_barrier(v.astype(jnp.bfloat16)).astype(jnp.float32)

@jax.custom_vjp
def low_back(v):
    return v

def low_keep(v):
    return (low(v), None)

def low_pass(kept, grad):
    return (grad,)

def back_keep(v):
    return (v, None)

def back_low(kept, grad):
    return (low(grad),)
low.defvjp(low_keep, low_pass)
low_back.defvjp(back_keep, back_low)
epsilon = 1e-05
neg_large = -1e+30

def exact_product(left_side, right_side):
    return jnp.dot(left_side, right_side, precision=lax.Precision.HIGHEST)

def layer_norm(values, gain_vector, shift_vector):
    average = lax.optimization_barrier(jnp.mean(values, axis=-1, keepdims=True))
    centred = values - average
    variance = lax.optimization_barrier(jnp.mean(centred * centred, axis=-1, keepdims=True))
    return centred * lax.rsqrt(variance + epsilon) * gain_vector + shift_vector

def gelu_tanh(values):
    return 0.5 * values * (1.0 + jnp.tanh(0.7978845608028654 * (values + 0.044715 * values * values * values)))

def softmax_rows(values):
    highest = lax.optimization_barrier(jnp.max(values, axis=-1, keepdims=True))
    raised = jnp.exp(values - highest)
    return raised / lax.optimization_barrier(jnp.sum(raised, axis=-1, keepdims=True))

def slot_numbers(block_routes, block_priority):
    same_expert = block_routes[:, None] == block_routes[None, :]
    earlier = block_priority[None, :] < block_priority[:, None]
    return lax.optimization_barrier(jnp.sum(jnp.logical_and(same_expert, earlier).astype(jnp.int32), axis=1))

def sequence_forward(params, seq_tokens, seq_segments, seq_routes, seq_priority):
    qkv_weight, out_weight, gain_first, shift_first, gain_second, shift_second, inner_weight, outer_weight, router_weight, expert_inner, expert_outer = params
    seq_length = seq_tokens.shape[0]
    model_width = seq_tokens.shape[1]
    float_type = seq_tokens.dtype
    first_low = low(layer_norm(seq_tokens, gain_first, shift_first))
    projected = low(low_back(exact_product(first_low, qkv_weight)))
    queries = projected[:, :model_width].reshape(seq_length, HEADS, HEAD_DIM)
    keys_all = projected[:, model_width:2 * model_width].reshape(seq_length, HEADS, HEAD_DIM)
    values_all = projected[:, 2 * model_width:].reshape(seq_length, HEADS, HEAD_DIM)
    positions = jnp.arange(seq_length, dtype=jnp.int32)
    scale_factor = 1.0 / math.sqrt(HEAD_DIM)

    def attend(block_number):
        block_first = (block_number * TOK_DEV).astype(jnp.int32)
        block_queries = lax.dynamic_slice_in_dim(queries, block_first, TOK_DEV)
        block_positions = lax.dynamic_slice_in_dim(positions, block_first, TOK_DEV)
        block_segments = lax.dynamic_slice_in_dim(seq_segments, block_first, TOK_DEV)
        scores = low_back(jnp.einsum('qhd,khd->hqk', block_queries, keys_all, precision=lax.Precision.HIGHEST) * scale_factor)
        visible = jnp.logical_and(positions[None, :] <= block_positions[:, None], seq_segments[None, :] == block_segments[:, None])
        weights = softmax_rows(jnp.where(visible[None], scores, neg_large))
        return jnp.einsum('hqk,khd->qhd', low(weights), values_all, precision=lax.Precision.HIGHEST)
    mixed_heads = lax.map(jax.checkpoint(attend), jnp.arange(N_CTX, dtype=jnp.int32))
    attended = low(low_back(mixed_heads.reshape(seq_length, model_width)))
    residual = seq_tokens + low_back(exact_product(attended, out_weight))
    second_low = low(layer_norm(residual, gain_second, shift_second))
    hidden_dense = low_back(exact_product(second_low, inner_weight))
    dense_out = exact_product(low(gelu_tanh(hidden_dense)), outer_weight)
    probabilities = softmax_rows(exact_product(second_low, router_weight))
    expert_count = router_weight.shape[1]
    chosen = (seq_routes[:, None] == jnp.arange(expert_count, dtype=jnp.int32)[None, :]).astype(float_type)
    gate_value = lax.optimization_barrier(jnp.sum(probabilities * chosen, axis=1))
    capacity = (9 * TOK_DEV + 8 * expert_count - 1) // (8 * expert_count)
    slot_index = jax.vmap(slot_numbers)(seq_routes.reshape(N_CTX, TOK_DEV), seq_priority).reshape(seq_length)
    kept_mask = slot_index < capacity
    kept_float = kept_mask.astype(float_type)
    block_ids = positions // TOK_DEV
    placement_index = jnp.where(kept_mask, seq_routes * (N_CTX * capacity) + block_ids * capacity + slot_index, 0).astype(jnp.int32)
    buffer_rows = jnp.zeros((expert_count * N_CTX * capacity, model_width), float_type)
    buffer_rows = buffer_rows.at[placement_index].add(second_low * kept_float[:, None])
    dispatched = low_back(buffer_rows.reshape(expert_count, N_CTX * capacity, model_width))
    expert_hidden = low_back(jnp.einsum('erd,edf->erf', dispatched, expert_inner, precision=lax.Precision.HIGHEST))
    expert_result = jnp.einsum('erf,efd->erd', low(gelu_tanh(expert_hidden)), expert_outer, precision=lax.Precision.HIGHEST)
    expert_result = low(low_back(expert_result)).reshape(expert_count * N_CTX * capacity, model_width)
    picked = expert_result[placement_index] * kept_float[:, None]
    return residual + dense_out + gate_value[:, None] * picked

def reference(tokens, qkv_weight, out_weight, norm1_gain, norm1_shift, norm2_gain, norm2_shift, inner_weight, outer_weight, router_weight, expert_inner, expert_outer, segments, routes, priority, cotangent):
    params = (qkv_weight.astype(jnp.float32), out_weight.astype(jnp.float32), norm1_gain.astype(jnp.float32), norm1_shift.astype(jnp.float32), norm2_gain.astype(jnp.float32), norm2_shift.astype(jnp.float32), inner_weight.astype(jnp.float32), outer_weight.astype(jnp.float32), router_weight.astype(jnp.float32), expert_inner.astype(jnp.float32), expert_outer.astype(jnp.float32))
    inputs_wide = tokens.astype(jnp.float32)
    route_ids = routes[:, :, 0]

    def whole_layer(layer_inputs, layer_params):

        def one_sequence(pieces):
            return sequence_forward(layer_params, pieces[0], pieces[1], pieces[2], pieces[3])
        return lax.map(jax.checkpoint(one_sequence), (layer_inputs, segments, route_ids, priority))
    output, pullback = jax.vjp(whole_layer, inputs_wide, params)
    d_inputs, d_params = pullback(cotangent.astype(jnp.float32))
    return (output.astype(jnp.bfloat16), d_inputs, d_params[0], d_params[1], d_params[2], d_params[3], d_params[4], d_params[5], d_params[6], d_params[7], d_params[8], d_params[9], d_params[10])
```

```python
import functools
import math

import jax
import jax.numpy as jnp
from jax import lax
from jax.experimental import pallas as pl
from jax.experimental.pallas import tpu as pltpu
from jax.sharding import PartitionSpec as P

HEADS = 16
HEAD_DIM = 64
AXES = ("dp", "ctx", "exp")
EPS = 1e-05
NEG = -1e30
GELU_A = 0.7978845608028654
GELU_B = 0.044715
F32 = jnp.float32
BF16 = jnp.bfloat16


def dot(a, b):
    return jnp.dot(a, b, preferred_element_type=F32)


def dot_nt(a, b):
    return lax.dot_general(a, b, (((1,), (1,)), ((), ())), preferred_element_type=F32)


def dot_tn(a, b):
    return lax.dot_general(a, b, (((0,), (0,)), ((), ())), preferred_element_type=F32)


def norm_parts(z):
    average = jnp.mean(z, axis=-1, keepdims=True)
    centred = z - average
    scale = lax.rsqrt(jnp.mean(centred * centred, axis=-1, keepdims=True) + EPS)
    return centred * scale, scale


def norm_back(grad, unit, scale, gain):
    w = grad * gain
    return scale * (
        w
        - jnp.mean(w, axis=-1, keepdims=True)
        - unit * jnp.mean(w * unit, axis=-1, keepdims=True)
    )


def gelu_pair(u):
    t = jnp.tanh(GELU_A * (u + GELU_B * u * u * u))
    value = 0.5 * u * (1.0 + t)
    slope = 0.5 * (1.0 + t) + 0.5 * u * (1.0 - t * t) * GELU_A * (1.0 + 3.0 * GELU_B * u * u)
    return value, slope


def softmax_rows(v):
    raised = jnp.exp(v - jnp.max(v, axis=-1, keepdims=True))
    return raised / jnp.sum(raised, axis=-1, keepdims=True)


def attention_fwd_kernel(block, q_ref, k_ref, v_ref, segrow_ref, segcol_ref, o_ref):
    length = q_ref.shape[0]
    scale = 1.0 / math.sqrt(HEAD_DIM)
    first_half = lax.broadcasted_iota(jnp.int32, (block, 2 * HEAD_DIM), 1) < HEAD_DIM
    for i in range(length // block):
        ext = (i + 1) * block
        rows = pl.ds(i * block, block)
        q = q_ref[rows, :]
        k = k_ref[pl.ds(0, ext), :]
        v = v_ref[pl.ds(0, ext), :]
        qpos = lax.broadcasted_iota(jnp.int32, (block, ext), 0) + i * block
        kpos = lax.broadcasted_iota(jnp.int32, (block, ext), 1)
        visible = jnp.logical_and(
            kpos <= qpos, segcol_ref[rows, :] == segrow_ref[:, pl.ds(0, ext)]
        )
        outs = []
        for half in range(2):
            mine = first_half if half == 0 else jnp.logical_not(first_half)
            qh = jnp.where(mine, q, jnp.zeros_like(q))
            s = jnp.where(visible, dot_nt(qh, k) * scale, NEG)
            p = jnp.exp(s - jnp.max(s, axis=1, keepdims=True))
            total = jnp.sum(p, axis=1, keepdims=True)
            outs.append(dot(p.astype(BF16), v) / total)
        o_ref[rows, :] = jnp.where(first_half, outs[0], outs[1]).astype(o_ref.dtype)


def attention_bwd_kernel(
    block, q_ref, k_ref, v_ref, do_ref, segrow_ref, segcol_ref, dq_ref, dk_ref, dv_ref, dk_acc, dv_acc
):
    length = q_ref.shape[0]
    scale = 1.0 / math.sqrt(HEAD_DIM)
    first_half = lax.broadcasted_iota(jnp.int32, (block, 2 * HEAD_DIM), 1) < HEAD_DIM
    dk_acc[...] = jnp.zeros_like(dk_acc)
    dv_acc[...] = jnp.zeros_like(dv_acc)
    for i in range(length // block):
        ext = (i + 1) * block
        rows = pl.ds(i * block, block)
        keys = pl.ds(0, ext)
        q = q_ref[rows, :]
        do = do_ref[rows, :]
        k = k_ref[keys, :]
        v = v_ref[keys, :]
        qpos = lax.broadcasted_iota(jnp.int32, (ext, block), 1) + i * block
        kpos = lax.broadcasted_iota(jnp.int32, (ext, block), 0)
        visible = jnp.logical_and(kpos <= qpos, segcol_ref[keys, :] == segrow_ref[:, rows])
        dq = []
        for half in range(2):
            mine = first_half if half == 0 else jnp.logical_not(first_half)
            qh = jnp.where(mine, q, jnp.zeros_like(q))
            doh = jnp.where(mine, do, jnp.zeros_like(do))
            s = jnp.where(visible, dot_nt(k, qh) * scale, NEG)
            p = jnp.exp(s - jnp.max(s, axis=0, keepdims=True))
            p = p * (1.0 / jnp.sum(p, axis=0, keepdims=True))
            dp = dot_nt(v, doh)
            delta = jnp.sum(p * dp, axis=0, keepdims=True)
            ds = (p * (dp - delta)).astype(BF16)
            dv_acc[keys, :] += dot(p.astype(BF16), doh)
            dk_acc[keys, :] += dot(ds, qh)
            dq.append(dot_tn(ds, k))
        dq_ref[rows, :] = (jnp.where(first_half, dq[0], dq[1]) * scale).astype(dq_ref.dtype)
    dk_ref[...] = (dk_acc[...] * scale).astype(dk_ref.dtype)
    dv_ref[...] = dv_acc[...].astype(dv_ref.dtype)


def attention_fwd(qkv, segs, block):
    length, width3 = qkv.shape
    width = width3 // 3
    pair = 2 * HEAD_DIM
    steps = width // pair
    return pl.pallas_call(
        functools.partial(attention_fwd_kernel, block),
        grid=(steps,),
        in_specs=[
            pl.BlockSpec((length, pair), lambda p: (0, p)),
            pl.BlockSpec((length, pair), lambda p: (0, steps + p)),
            pl.BlockSpec((length, pair), lambda p: (0, 2 * steps + p)),
            pl.BlockSpec((1, length), lambda p: (0, 0)),
            pl.BlockSpec((length, 1), lambda p: (0, 0)),
        ],
        out_specs=pl.BlockSpec((length, pair), lambda p: (0, p)),
        out_shape=jax.ShapeDtypeStruct((length, width), BF16),
        compiler_params=pltpu.CompilerParams(vmem_limit_bytes=48 * 1024 * 1024),
        cost_estimate=pl.CostEstimate(
            flops=8 * length * length * width, bytes_accessed=8 * length * width,
            transcendentals=length * length * width // HEAD_DIM // 2,
        ),
    )(qkv, qkv, qkv, segs[None, :], segs[:, None])


def attention_bwd(qkv, d_out, segs, block):
    length, width3 = qkv.shape
    width = width3 // 3
    pair = 2 * HEAD_DIM
    steps = width // pair
    out = jax.ShapeDtypeStruct((length, width), BF16)
    spec = pl.BlockSpec((length, pair), lambda p: (0, p))
    return pl.pallas_call(
        functools.partial(attention_bwd_kernel, block),
        grid=(steps,),
        in_specs=[
            spec,
            pl.BlockSpec((length, pair), lambda p: (0, steps + p)),
            pl.BlockSpec((length, pair), lambda p: (0, 2 * steps + p)),
            spec,
            pl.BlockSpec((1, length), lambda p: (0, 0)),
            pl.BlockSpec((length, 1), lambda p: (0, 0)),
        ],
        out_specs=[spec, spec, spec],
        out_shape=[out, out, out],
        scratch_shapes=[pltpu.VMEM((length, pair), F32), pltpu.VMEM((length, pair), F32)],
        compiler_params=pltpu.CompilerParams(vmem_limit_bytes=48 * 1024 * 1024),
        cost_estimate=pl.CostEstimate(
            flops=20 * length * length * width, bytes_accessed=14 * length * width,
            transcendentals=length * length * width // HEAD_DIM // 2,
        ),
    )(qkv, qkv, qkv, d_out, segs[None, :], segs[:, None])


def solution(mesh):
    nd, nc, ne = (mesh.shape[a] for a in AXES)
    ndev = nd * nc * ne
    bits_of = lambda n: [1 << b for b in range(n.bit_length() - 1)]
    low_bits, all_bits = bits_of(nc), bits_of(ne)
    high_bits = [b for b in all_bits if b not in low_bits]


    def send(x, target):
        pairs = []
        for d in range(nd):
            for c in range(nc):
                for e in range(ne):
                    to = target(d, c, e)
                    if to is not None:
                        pairs.append(((d * nc + c) * ne + e, (to[0] * nc + to[1]) * ne + to[2]))
        return lax.ppermute(x, AXES, pairs)

    def swap_exp(x, bit):
        return send(x, lambda d, c, e: (d, c, e ^ bit))

    def swap_dp(x):
        return send(x, lambda d, c, e: (d ^ 1, c, e))

    def swap_seq(x):
        return send(x, lambda d, c, e: (d, e % nc, e - e % nc + c))

    def my_bit(bit):
        return (lax.axis_index("exp") // bit) % 2

    def ordered(mine, other, index, axis):
        return jnp.where(
            index == 0, jnp.stack([mine, other], axis), jnp.stack([other, mine], axis)
        )

    def gather_exp(x, bits):
        out = x[None]
        for bit in reversed(bits):
            out = ordered(out, swap_exp(out, bit), my_bit(bit), 1)
            out = out.reshape((-1,) + x.shape)
        return out

    def gather_exp_rel(x, bits):
        out = x[None]
        for bit in reversed(bits):
            out = jnp.stack([out, swap_exp(out, bit)], 1).reshape((-1,) + x.shape)
        return out

    def split_bit(x, position, count):
        shape = x.shape
        return x.reshape((shape[0] >> (position + 1), 2, 1 << position) + shape[1:])

    def scatter_exp_rel(parts, bits):
        for bit in bits:
            pairs = parts.reshape((-1, 2) + parts.shape[1:])
            parts = pairs[:, 0].astype(F32) + swap_exp(pairs[:, 1].astype(BF16), bit).astype(F32)
        return parts[0]

    def scatter_exp(parts, bits):
        for bit in bits:
            pairs = parts.reshape((-1, 2) + parts.shape[1:])
            mine = my_bit(bit)
            keep = lax.dynamic_index_in_dim(pairs, mine, 1, keepdims=False)
            away = lax.dynamic_index_in_dim(pairs, 1 - mine, 1, keepdims=False)
            parts = keep.astype(F32) + swap_exp(away.astype(BF16), bit).astype(F32)
        return parts[0]

    def trade_exp_rel(parts, bits):
        for position, bit in enumerate(bits):
            pairs = split_bit(parts, position, len(bits))
            parts = jnp.stack([pairs[:, 0], swap_exp(pairs[:, 1], bit)], 1).reshape(parts.shape)
        return parts

    def trade_exp(parts, bits):
        for position, bit in enumerate(bits):
            pairs = split_bit(parts, position, len(bits))
            mine = my_bit(bit)
            keep = lax.dynamic_index_in_dim(pairs, mine, 1, keepdims=False)
            away = lax.dynamic_index_in_dim(pairs, 1 - mine, 1, keepdims=False)
            parts = ordered(keep, swap_exp(away, bit), mine, 1).reshape(parts.shape)
        return parts

    def line_steps(x):
        below, above, up, down = [], [], x, x
        for k in range(1, nc):
            up = send(up, lambda d, c, e: (d, c + 1, e) if k - 1 <= c < nc - 1 else None)
            down = send(down, lambda d, c, e: (d, c - 1, e) if 0 < c <= nc - k else None)
            below.append(up)
            above.append(down)
        return below, above

    def line_order(own, below, above):
        stack = jnp.stack(below[::-1] + [own] + above)
        return lax.dynamic_slice_in_dim(stack, nc - 1 - lax.axis_index("ctx"), nc)

    def gather_line(x):
        below, above = line_steps(x)
        return line_order(x, below, above)

    def gather_plane(x):
        below, above = line_steps(x)
        mine = line_order(x, below, above)
        other = line_order(
            swap_dp(x),
            [send(v, lambda d, c, e: (d ^ 1, c, e) if c >= k + 1 else None) for k, v in enumerate(below)],
            [send(v, lambda d, c, e: (d ^ 1, c, e) if c < nc - 1 - k else None) for k, v in enumerate(above)],
        )
        return ordered(mine, other, lax.axis_index("dp"), 0)

    def scatter_line(parts):
        c_here = lax.axis_index("ctx")

        def part(j):
            return lax.dynamic_index_in_dim(parts, jnp.clip(j, 0, nc - 1), 0, keepdims=False)

        up = down = None
        for t in range(1, nc):
            away = nc - t
            high, low = part(c_here + away), part(c_here - away)
            if up is not None:
                high = high.astype(F32) + up.astype(F32)
                low = low.astype(F32) + down.astype(F32)
            up = send(high.astype(BF16), lambda d, c, e: (d, c + 1, e) if c + away < nc else None)
            down = send(low.astype(BF16), lambda d, c, e: (d, c - 1, e) if c - away >= 0 else None)
        return part(c_here).astype(F32) + up.astype(F32) + down.astype(F32)

    def scatter_plane(parts):
        d_here = lax.axis_index("dp")
        keep = lax.dynamic_index_in_dim(parts, d_here, 0, keepdims=False)
        away = lax.dynamic_index_in_dim(parts, 1 - d_here, 0, keepdims=False)
        return scatter_line(keep.astype(F32) + swap_dp(away.astype(BF16)).astype(F32))

    def per_device(
        tokens, qkv_weight, out_weight, norm1_gain, norm1_shift, norm2_gain, norm2_shift,
        inner_weight, outer_weight, router_weight, expert_inner, expert_outer,
        segments, routes, priority, cotangent,
    ):
        rows, width = tokens.shape[1:]
        length = segments.shape[1]
        rw = qkv_weight.shape[0]
        ff_rows = outer_weight.shape[0]
        nplane = nd * nc
        e_here = lax.axis_index("exp")
        group = width // nc

        x_low = swap_seq(tokens[0])
        ints = jnp.concatenate([segments[0], routes[0, :, 0], priority[0, 0]])
        ints = swap_seq(ints.reshape(-1, 128)).reshape(-1)
        segs, route, order = ints[:length], ints[length : length + rows], ints[length + rows :]

        small = jnp.concatenate(
            [norm1_gain, norm1_shift, norm2_gain, norm2_shift, router_weight.reshape(-1)]
        )
        small = lax.all_to_all(
            jnp.broadcast_to(small[None], (ndev,) + small.shape), AXES, 0, 0, tiled=True
        )
        gain1, shift1, gain2, shift2 = (
            small[:, i * rw : (i + 1) * rw].reshape(width).astype(F32) for i in range(4)
        )
        router = small[:, 4 * rw :].reshape(width, ne)

        qkv_part = jnp.moveaxis(qkv_weight.reshape(rw, 3, nc, group), 2, 0)
        qkv_part = trade_exp(qkv_part.reshape(nc, rw, 3 * group), low_bits)
        qkv_part = gather_exp(qkv_part.reshape(nc * rw, 3 * group), high_bits)
        qkv_rows = width // nplane
        qkv_flat = qkv_part.reshape(-1, width)
        bundle = gather_plane(jnp.concatenate([qkv_flat, out_weight]))
        w_qkv = bundle[:, :, : qkv_flat.shape[0]].reshape(width, 3 * group)
        w_out = gather_exp(bundle[:, :, qkv_flat.shape[0] :], all_bits)
        w_out = jnp.moveaxis(w_out, 0, 2).reshape(width, width)

        inner_part = jnp.moveaxis(inner_weight.reshape(rw, nplane, ne, ff_rows), 2, 0)
        inner_part = trade_exp(inner_part.reshape(ne, rw, nplane * ff_rows), all_bits)
        inner_flat = inner_part.reshape(-1, width)
        bundle = gather_plane(jnp.concatenate([inner_flat, outer_weight]))
        ff = nplane * ff_rows
        w_inner = bundle[:, :, : inner_flat.shape[0]].reshape(width, ff)
        w_outer = bundle[:, :, inner_flat.shape[0] :].reshape(ff, width)

        e_in_own, e_out_own = expert_inner[0], expert_outer[0]
        e_in = jnp.concatenate([e_in_own, swap_dp(e_in_own)], axis=1)
        e_out = jnp.concatenate([e_out_own, swap_dp(e_out_own)], axis=0)
        half = e_out_own.shape[0]

        x = x_low.astype(F32)
        unit1, scale1 = norm_parts(x)
        normed = (unit1 * gain1 + shift1).astype(BF16)
        normed_all = gather_exp(normed, low_bits).reshape(length, width)
        qkv = dot(normed_all, w_qkv).astype(BF16)
        mixed = attention_fwd(qkv, segs, rows)
        attended = trade_exp(mixed.reshape(nc, rows, group), low_bits)
        attended = jnp.moveaxis(attended, 0, 1).reshape(rows, width)
        residual = x + dot(attended, w_out)
        unit2, scale2 = norm_parts(residual)
        normed2 = (unit2 * gain2 + shift2).astype(BF16)

        cot_low = swap_seq(cotangent[0])
        cot = cot_low.astype(F32)
        capacity = (9 * rows + 8 * ne - 1) // (8 * ne)
        same = route[:, None] == route[None, :]
        earlier = order[None, :] < order[:, None]
        slot = jnp.sum(jnp.logical_and(same, earlier).astype(jnp.int32), axis=1)
        place = jnp.where(slot < capacity, (route ^ e_here) * capacity + slot, -1)
        slots = ne * capacity
        table = (jnp.arange(slots, dtype=jnp.int32)[:, None] == place[None, :]).astype(BF16)

        def to_experts(v):
            out = dot(table, v).astype(BF16).reshape(ne, capacity, width)
            out = trade_exp_rel(out, all_bits).reshape(slots, width)
            return gather_line(out).reshape(nc * slots, width)

        def from_experts(v):
            back = scatter_line(v.reshape(nc, slots, width)).astype(BF16)
            back = trade_exp_rel(back.reshape(ne, capacity, width), all_bits)
            return dot_tn(table, back.reshape(slots, width))

        e_cot = to_experts(cot_low)
        e_x = to_experts(normed2)

        cot_all = gather_exp_rel(cot_low, all_bits).reshape(ne * rows, width)
        n2_all = gather_exp_rel(normed2, all_bits).reshape(ne * rows, width)
        act, slope = gelu_pair(dot(n2_all, w_inner))
        act = act.astype(BF16)
        d_hidden = (dot_nt(cot_all, w_outer) * slope).astype(BF16)
        dense_part = dot(act, w_outer).reshape(ne, rows, width)
        d_n2_part = dot_nt(d_hidden, w_inner).reshape(ne, rows, width)
        dense = scatter_exp_rel(dense_part, all_bits)
        d_n2_dense = scatter_exp_rel(d_n2_part, all_bits)
        d_outer = dot_tn(act, cot_all)
        d_inner = dot_tn(n2_all, d_hidden)

        e_probs = softmax_rows(dot(e_x, router))
        mine = (jnp.arange(ne, dtype=jnp.int32) == e_here).astype(F32)[None, :]
        e_gate = jnp.sum(e_probs * mine, axis=1, keepdims=True)
        e_grad = (e_gate * e_cot.astype(F32)).astype(BF16)
        e_act, e_slope = gelu_pair(dot(e_x, e_in))
        e_act = e_act.astype(BF16)
        e_result = dot(e_act, e_out)
        d_e_hidden = (dot_nt(e_grad, e_out) * e_slope).astype(BF16)
        d_gate = jnp.sum(e_cot.astype(F32) * e_result, axis=1, keepdims=True)
        d_logits = d_gate * e_probs * (mine - e_gate)
        d_e_x = dot_nt(d_e_hidden, e_in) + dot_nt(d_logits, router.astype(F32))
        d_router = dot_tn(e_x.astype(F32), d_logits)
        d_e_out = dot_tn(e_act, e_grad)
        d_e_in = dot_tn(e_x, d_e_hidden)
        g_e_in = d_e_in[:, :half] + swap_dp(d_e_in[:, half:].astype(BF16)).astype(F32)
        g_e_out = d_e_out[:half] + swap_dp(d_e_out[half:].astype(BF16)).astype(F32)

        d_n2 = d_n2_dense + from_experts(d_e_x)
        picked = from_experts(e_result)
        probs = softmax_rows(dot(normed2, router))
        chosen = (route[:, None] == jnp.arange(ne, dtype=jnp.int32)[None, :]).astype(F32)
        gate = jnp.sum(probs * chosen, axis=1, keepdims=True)
        output = swap_seq((residual + dense + gate * picked).astype(BF16))

        d_gain2 = jnp.sum(d_n2 * unit2, axis=0)
        d_shift2 = jnp.sum(d_n2, axis=0)
        d_residual = cot + norm_back(d_n2, unit2, scale2, gain2)
        d_branch = d_residual.astype(BF16)
        d_out = dot_tn(attended, d_branch)
        d_att = dot_nt(d_branch, w_out).astype(BF16)
        d_att = jnp.moveaxis(d_att.reshape(rows, nc, group), 1, 0)
        d_mixed = trade_exp(d_att, low_bits).reshape(length, group)
        d_qkv = jnp.concatenate(attention_bwd(qkv, d_mixed, segs, rows), axis=1)
        d_normed = dot_nt(d_qkv, w_qkv).reshape(nc, rows, width)
        d_normed = scatter_exp(d_normed, low_bits)
        d_w_qkv = dot_tn(normed_all, d_qkv)
        d_gain1 = jnp.sum(d_normed * unit1, axis=0)
        d_shift1 = jnp.sum(d_normed, axis=0)
        d_tokens = d_residual + norm_back(d_normed, unit1, scale1, gain1)
        d_tokens = swap_seq(d_tokens.astype(BF16)).astype(F32)

        bundle = jnp.concatenate(
            [d_inner.reshape(nd, nc, -1, width), d_outer.reshape(nd, nc, -1, width)], axis=2
        )
        bundle = scatter_plane(bundle)
        g_outer = bundle[inner_flat.shape[0] :]
        g_inner = bundle[: inner_flat.shape[0]].astype(BF16).reshape(ne, rw, ff)
        g_inner = trade_exp(g_inner, all_bits).reshape(ne, rw, nplane, ff_rows)
        g_inner = jnp.transpose(g_inner, (1, 2, 0, 3)).reshape(rw, -1).astype(F32)

        d_out = jnp.moveaxis(d_out.reshape(nplane, ne, rw, width), 1, 0)
        d_out = scatter_exp(d_out, all_bits).reshape(nd, nc, rw, width)
        bundle = jnp.concatenate([d_w_qkv.reshape(nd, nc, -1, width), d_out], axis=2)
        bundle = scatter_plane(bundle)
        g_out = bundle[qkv_flat.shape[0] :]
        g_qkv = bundle[: qkv_flat.shape[0]].reshape(-1, nc * rw, 3 * group)
        g_qkv = scatter_exp(g_qkv, high_bits).astype(BF16).reshape(nc, rw, 3 * group)
        g_qkv = trade_exp(g_qkv, low_bits).reshape(nc, rw, 3, group)
        g_qkv = jnp.transpose(g_qkv, (1, 2, 0, 3)).reshape(rw, 3 * width).astype(F32)

        small = jnp.concatenate([jnp.stack([d_gain1, d_shift1, d_gain2, d_shift2], 1), d_router], 1)
        small = lax.all_to_all(small.reshape(ndev, -1), AXES, 0, 0, tiled=True)
        small = jnp.sum(small, axis=0).reshape(rw, 4 + ne)

        return (
            output[None], d_tokens[None], g_qkv, g_out,
            small[:, 0], small[:, 1], small[:, 2], small[:, 3],
            g_inner, g_outer, small[:, 4:], g_e_in[None], g_e_out[None],
        )

    rest = ("dp", "ctx", "exp")
    seq = P(("dp", "exp"), "ctx", None)
    in_specs = (
        seq, P(rest, None), P(rest, None), P(rest), P(rest), P(rest), P(rest),
        P(rest, None), P(rest, None), P(rest, None),
        P("exp", None, ("dp", "ctx")), P("exp", ("dp", "ctx"), None),
        P(("dp", "exp"), None), seq, seq, seq,
    )
    out_specs = (
        seq, seq, P(rest, None), P(rest, None), P(rest), P(rest), P(rest), P(rest),
        P(rest, None), P(rest, None), P(rest, None),
        P("exp", None, ("dp", "ctx")), P("exp", ("dp", "ctx"), None),
    )
    return jax.shard_map(
        per_device, mesh=mesh, in_specs=in_specs, out_specs=out_specs, check_vma=False
    )
```

```python
import functools
import math

import jax
import jax.numpy as jnp
from jax import lax
from jax.experimental import pallas as pl
from jax.experimental.pallas import tpu as pltpu
from jax.sharding import PartitionSpec as P

HEADS = 16
HEAD_DIM = 64
AXES = ("dp", "ctx", "exp")
EPS = 1e-05
NEG = -1e30
GELU_A = 0.7978845608028654
GELU_B = 0.044715
F32 = jnp.float32
BF16 = jnp.bfloat16


def dot(a, b):
    return jnp.dot(a, b, preferred_element_type=F32)


def dot_nt(a, b):
    return lax.dot_general(a, b, (((1,), (1,)), ((), ())), preferred_element_type=F32)


def dot_tn(a, b):
    return lax.dot_general(a, b, (((0,), (0,)), ((), ())), preferred_element_type=F32)


def norm_parts(z):
    average = jnp.mean(z, axis=-1, keepdims=True)
    centred = z - average
    scale = lax.rsqrt(jnp.mean(centred * centred, axis=-1, keepdims=True) + EPS)
    return centred * scale, scale


def norm_back(grad, unit, scale, gain):
    w = grad * gain
    return scale * (
        w
        - jnp.mean(w, axis=-1, keepdims=True)
        - unit * jnp.mean(w * unit, axis=-1, keepdims=True)
    )


def gelu_pair(u):
    t = jnp.tanh(GELU_A * (u + GELU_B * u * u * u))
    value = 0.5 * u * (1.0 + t)
    slope = 0.5 * (1.0 + t) + 0.5 * u * (1.0 - t * t) * GELU_A * (1.0 + 3.0 * GELU_B * u * u)
    return value, slope


def softmax_rows(v):
    raised = jnp.exp(v - jnp.max(v, axis=-1, keepdims=True))
    return raised / jnp.sum(raised, axis=-1, keepdims=True)


def attention_fwd_kernel(block, q_ref, k_ref, v_ref, segrow_ref, segcol_ref, o_ref):
    length = q_ref.shape[0]
    scale = 1.0 / math.sqrt(HEAD_DIM)
    first_half = lax.broadcasted_iota(jnp.int32, (block, 2 * HEAD_DIM), 1) < HEAD_DIM
    for i in range(length // block):
        ext = (i + 1) * block
        rows = pl.ds(i * block, block)
        q = q_ref[rows, :]
        k = k_ref[pl.ds(0, ext), :]
        v = v_ref[pl.ds(0, ext), :]
        qpos = lax.broadcasted_iota(jnp.int32, (block, ext), 0) + i * block
        kpos = lax.broadcasted_iota(jnp.int32, (block, ext), 1)
        visible = jnp.logical_and(
            kpos <= qpos, segcol_ref[rows, :] == segrow_ref[:, pl.ds(0, ext)]
        )
        outs = []
        for half in range(2):
            mine = first_half if half == 0 else jnp.logical_not(first_half)
            qh = jnp.where(mine, q, jnp.zeros_like(q))
            s = jnp.where(visible, dot_nt(qh, k) * scale, NEG)
            p = jnp.exp(s - jnp.max(s, axis=1, keepdims=True))
            total = jnp.sum(p, axis=1, keepdims=True)
            outs.append(dot(p.astype(BF16), v) / total)
        o_ref[rows, :] = jnp.where(first_half, outs[0], outs[1]).astype(o_ref.dtype)


def attention_bwd_kernel(
    block, q_ref, k_ref, v_ref, do_ref, segrow_ref, segcol_ref, dq_ref, dk_ref, dv_ref, dk_acc, dv_acc
):
    length = q_ref.shape[0]
    scale = 1.0 / math.sqrt(HEAD_DIM)
    first_half = lax.broadcasted_iota(jnp.int32, (block, 2 * HEAD_DIM), 1) < HEAD_DIM
    dk_acc[...] = jnp.zeros_like(dk_acc)
    dv_acc[...] = jnp.zeros_like(dv_acc)
    for i in range(length // block):
        ext = (i + 1) * block
        rows = pl.ds(i * block, block)
        keys = pl.ds(0, ext)
        q = q_ref[rows, :]
        do = do_ref[rows, :]
        k = k_ref[keys, :]
        v = v_ref[keys, :]
        qpos = lax.broadcasted_iota(jnp.int32, (ext, block), 1) + i * block
        kpos = lax.broadcasted_iota(jnp.int32, (ext, block), 0)
        visible = jnp.logical_and(kpos <= qpos, segcol_ref[keys, :] == segrow_ref[:, rows])
        dq = []
        for half in range(2):
            mine = first_half if half == 0 else jnp.logical_not(first_half)
            qh = jnp.where(mine, q, jnp.zeros_like(q))
            doh = jnp.where(mine, do, jnp.zeros_like(do))
            s = jnp.where(visible, dot_nt(k, qh) * scale, NEG)
            p = jnp.exp(s - jnp.max(s, axis=0, keepdims=True))
            p = p * (1.0 / jnp.sum(p, axis=0, keepdims=True))
            dp = dot_nt(v, doh)
            delta = jnp.sum(p * dp, axis=0, keepdims=True)
            ds = (p * (dp - delta)).astype(BF16)
            dv_acc[keys, :] += dot(p.astype(BF16), doh)
            dk_acc[keys, :] += dot(ds, qh)
            dq.append(dot_tn(ds, k))
        dq_ref[rows, :] = (jnp.where(first_half, dq[0], dq[1]) * scale).astype(dq_ref.dtype)
    dk_ref[...] = (dk_acc[...] * scale).astype(dk_ref.dtype)
    dv_ref[...] = dv_acc[...].astype(dv_ref.dtype)


def attention_fwd(qkv, segs, block):
    length, width3 = qkv.shape
    width = width3 // 3
    pair = 2 * HEAD_DIM
    steps = width // pair
    return pl.pallas_call(
        functools.partial(attention_fwd_kernel, block),
        grid=(steps,),
        in_specs=[
            pl.BlockSpec((length, pair), lambda p: (0, p)),
            pl.BlockSpec((length, pair), lambda p: (0, steps + p)),
            pl.BlockSpec((length, pair), lambda p: (0, 2 * steps + p)),
            pl.BlockSpec((1, length), lambda p: (0, 0)),
            pl.BlockSpec((length, 1), lambda p: (0, 0)),
        ],
        out_specs=pl.BlockSpec((length, pair), lambda p: (0, p)),
        out_shape=jax.ShapeDtypeStruct((length, width), BF16),
        compiler_params=pltpu.CompilerParams(vmem_limit_bytes=48 * 1024 * 1024),
        cost_estimate=pl.CostEstimate(
            flops=8 * length * length * width, bytes_accessed=8 * length * width,
            transcendentals=length * length * width // HEAD_DIM // 2,
        ),
    )(qkv, qkv, qkv, segs[None, :], segs[:, None])


def attention_bwd(qkv, d_out, segs, block):
    length, width3 = qkv.shape
    width = width3 // 3
    pair = 2 * HEAD_DIM
    steps = width // pair
    out = jax.ShapeDtypeStruct((length, width), BF16)
    spec = pl.BlockSpec((length, pair), lambda p: (0, p))
    return pl.pallas_call(
        functools.partial(attention_bwd_kernel, block),
        grid=(steps,),
        in_specs=[
            spec,
            pl.BlockSpec((length, pair), lambda p: (0, steps + p)),
            pl.BlockSpec((length, pair), lambda p: (0, 2 * steps + p)),
            spec,
            pl.BlockSpec((1, length), lambda p: (0, 0)),
            pl.BlockSpec((length, 1), lambda p: (0, 0)),
        ],
        out_specs=[spec, spec, spec],
        out_shape=[out, out, out],
        scratch_shapes=[pltpu.VMEM((length, pair), F32), pltpu.VMEM((length, pair), F32)],
        compiler_params=pltpu.CompilerParams(vmem_limit_bytes=48 * 1024 * 1024),
        cost_estimate=pl.CostEstimate(
            flops=20 * length * length * width, bytes_accessed=14 * length * width,
            transcendentals=length * length * width // HEAD_DIM // 2,
        ),
    )(qkv, qkv, qkv, d_out, segs[None, :], segs[:, None])


def dense_kernel(
    rows, step, x_ref, g_ref, wi_ref, wo_ref, both_ref, dwi_ref, dwo_ref, act_ref, dh_ref
):
    @pl.loop(0, x_ref.shape[0] // rows)
    def _(t):
        r = pl.ds(pl.multiple_of(t * rows, rows), rows)
        act, slope = gelu_pair(dot(x_ref[r, :], wi_ref[...]))
        act = act.astype(BF16)
        dh = (dot_nt(g_ref[r, :], wo_ref[...]) * slope).astype(BF16)
        act_ref[r, :] = act
        dh_ref[r, :] = dh
        both_ref[t % 2, 0, t // 2] = dot(act, wo_ref[...]).astype(BF16)
        both_ref[t % 2, 1, t // 2] = dot_nt(dh, wi_ref[...]).astype(BF16)

    @pl.loop(0, act_ref.shape[1] // min(step, act_ref.shape[1]))
    def _(f):
        size = min(step, act_ref.shape[1])
        c = pl.ds(pl.multiple_of(f * size, size), size)
        dwo_ref[c, :] = dot_tn(act_ref[:, c], g_ref[...]).astype(BF16)

    @pl.loop(0, x_ref.shape[1] // step)
    def _(d):
        c = pl.ds(pl.multiple_of(d * step, step), step)
        dwi_ref[c, :] = dot_tn(x_ref[:, c], dh_ref[...]).astype(BF16)


def dense_block(x, g, w_inner, w_outer, rows):
    tokens, width = x.shape
    ff = w_inner.shape[1]
    return pl.pallas_call(
        functools.partial(dense_kernel, rows, 512),
        out_shape=[
            jax.ShapeDtypeStruct((2, 2, tokens // rows // 2, rows, width), BF16),
            jax.ShapeDtypeStruct((width, ff), BF16),
            jax.ShapeDtypeStruct((ff, width), BF16),
        ],
        scratch_shapes=[pltpu.VMEM((tokens, ff), BF16), pltpu.VMEM((tokens, ff), BF16)],
        compiler_params=pltpu.CompilerParams(vmem_limit_bytes=56 * 1024 * 1024),
        cost_estimate=pl.CostEstimate(
            flops=12 * tokens * width * ff,
            bytes_accessed=8 * tokens * width + 8 * width * ff,
            transcendentals=tokens * ff,
        ),
    )(x, g, w_inner, w_outer)


def expert_kernel(
    rows, step, ne, x_ref, c_ref, wi_ref, wo_ref, mine_ref,
    y_ref, dx_ref, dwi_own_ref, dwi_other_ref, dwo_own_ref, dwo_other_ref, drouter_ref,
    act_ref, dh_ref, g_ref,
):
    ff = wo_ref.shape[0]
    half = ff // 2
    mine = mine_ref[...]
    lanes = lax.broadcasted_iota(jnp.int32, (rows, mine.shape[1]), 1)

    @pl.loop(0, x_ref.shape[0] // rows)
    def _(t):
        r = pl.ds(pl.multiple_of(t * rows, rows), rows)
        hidden = dot(x_ref[r, :], wi_ref[...])
        logits = jnp.where(lanes < ne, hidden[:, ff:], NEG)
        raised = jnp.exp(logits - jnp.max(logits, axis=1, keepdims=True))
        probs = raised / jnp.sum(raised, axis=1, keepdims=True)
        gate = jnp.sum(probs * mine, axis=1, keepdims=True)
        act, slope = gelu_pair(hidden[:, :ff])
        act = act.astype(BF16)
        cot = c_ref[r, :].astype(F32)
        grad = (gate * cot).astype(BF16)
        dh = (dot_nt(grad, wo_ref[...]) * slope).astype(BF16)
        result = dot(act, wo_ref[...])
        d_gate = jnp.sum(cot * result, axis=1, keepdims=True)
        act_ref[r, :] = act
        g_ref[r, :] = grad
        dh_ref[r, :ff] = dh
        dh_ref[r, ff:] = (d_gate * probs * (mine - gate)).astype(BF16)
        y_ref[r, :] = result.astype(BF16)
        dx_ref[r, :] = dot_nt(dh_ref[r, :], wi_ref[...]).astype(BF16)

    dwo_own_ref[...] = dot_tn(act_ref[:, :half], g_ref[...])
    dwo_other_ref[...] = dot_tn(act_ref[:, half:], g_ref[...]).astype(BF16)

    @pl.loop(0, x_ref.shape[1] // step)
    def _(d):
        c = pl.ds(pl.multiple_of(d * step, step), step)
        grad = dot_tn(x_ref[:, c], dh_ref[...])
        dwi_own_ref[c, :] = grad[:, :half]
        dwi_other_ref[c, :] = grad[:, half:ff].astype(BF16)
        drouter_ref[c, :] = grad[:, ff:]


def expert_block(x, cot, w_in, w_out, mine, rows, ne):
    tokens, width = x.shape
    ff = w_out.shape[0]
    pad = w_in.shape[1] - ff
    half = ff // 2
    s = jax.ShapeDtypeStruct
    return pl.pallas_call(
        functools.partial(expert_kernel, rows, 256, ne),
        out_shape=[
            s((tokens, width), BF16), s((tokens, width), BF16),
            s((width, half), F32), s((width, half), BF16),
            s((half, width), F32), s((half, width), BF16),
            s((width, pad), F32),
        ],
        scratch_shapes=[
            pltpu.VMEM((tokens, ff), BF16),
            pltpu.VMEM((tokens, ff + pad), BF16),
            pltpu.VMEM((tokens, width), BF16),
        ],
        compiler_params=pltpu.CompilerParams(vmem_limit_bytes=56 * 1024 * 1024),
        cost_estimate=pl.CostEstimate(
            flops=12 * tokens * width * ff,
            bytes_accessed=8 * tokens * width + 10 * width * ff,
            transcendentals=tokens * ff,
        ),
    )(x, cot, w_in, w_out, mine)


def solution(mesh):
    nd, nc, ne = (mesh.shape[a] for a in AXES)
    ndev = nd * nc * ne
    bits_of = lambda n: [1 << b for b in range(n.bit_length() - 1)]
    low_bits, all_bits = bits_of(nc), bits_of(ne)
    high_bits = [b for b in all_bits if b not in low_bits]


    def send(x, target):
        pairs = []
        for d in range(nd):
            for c in range(nc):
                for e in range(ne):
                    to = target(d, c, e)
                    if to is not None:
                        pairs.append(((d * nc + c) * ne + e, (to[0] * nc + to[1]) * ne + to[2]))
        return lax.ppermute(x, AXES, pairs)

    def swap_exp(x, bit):
        return send(x, lambda d, c, e: (d, c, e ^ bit))

    def swap_dp(x):
        return send(x, lambda d, c, e: (d ^ 1, c, e))

    def reverse(i):
        return int(format(i, "b").zfill(len(low_bits))[::-1], 2)

    def to_seq(x):
        return send(x, lambda d, c, e: (d, reverse(e % nc), e - e % nc + c))

    def from_seq(x):
        return send(x, lambda d, c, e: (d, e % nc, e - e % nc + reverse(c)))

    def my_bit(bit):
        return (lax.axis_index("exp") // bit) % 2

    def ordered(mine, other, index, axis):
        return jnp.where(
            index == 0, jnp.stack([mine, other], axis), jnp.stack([other, mine], axis)
        )

    def gather_exp(x, bits):
        out = x[None]
        for bit in reversed(bits):
            out = ordered(out, swap_exp(out, bit), my_bit(bit), 1)
            out = out.reshape((-1,) + x.shape)
        return out

    def gather_exp_rel(x, bits):
        out = x[None]
        for bit in reversed(bits):
            out = jnp.stack([out, swap_exp(out, bit)], 1).reshape((-1,) + x.shape)
        return out

    def split_bit(x, position, count):
        shape = x.shape
        return x.reshape((shape[0] >> (position + 1), 2, 1 << position) + shape[1:])

    def scatter_exp_rel(parts, bits):
        for bit in bits:
            pairs = parts.reshape((-1, 2) + parts.shape[1:])
            parts = pairs[:, 0].astype(F32) + swap_exp(pairs[:, 1].astype(BF16), bit).astype(F32)
        return parts[0]

    def scatter_exp(parts, bits):
        for bit in bits:
            pairs = parts.reshape((-1, 2) + parts.shape[1:])
            mine = my_bit(bit)
            keep = lax.dynamic_index_in_dim(pairs, mine, 1, keepdims=False)
            away = lax.dynamic_index_in_dim(pairs, 1 - mine, 1, keepdims=False)
            parts = keep.astype(F32) + swap_exp(away.astype(BF16), bit).astype(F32)
        return parts[0]

    def trade_exp_rel(parts, bits):
        for position, bit in enumerate(bits):
            pairs = split_bit(parts, position, len(bits))
            parts = jnp.stack([pairs[:, 0], swap_exp(pairs[:, 1], bit)], 1).reshape(parts.shape)
        return parts

    def trade_exp(parts, bits):
        for position, bit in enumerate(bits):
            pairs = split_bit(parts, position, len(bits))
            mine = my_bit(bit)
            keep = lax.dynamic_index_in_dim(pairs, mine, 1, keepdims=False)
            away = lax.dynamic_index_in_dim(pairs, 1 - mine, 1, keepdims=False)
            parts = ordered(keep, swap_exp(away, bit), mine, 1).reshape(parts.shape)
        return parts

    def gather_ctx(x):
        return lax.all_to_all(
            jnp.broadcast_to(x[None], (nc,) + x.shape), "ctx", 0, 0, tiled=True
        )

    def gather_plane(x):
        mine = gather_ctx(x)
        return ordered(mine, swap_dp(mine), lax.axis_index("dp"), 0)

    def scatter_ctx(parts):
        parts = lax.all_to_all(parts.astype(BF16), "ctx", 0, 0, tiled=True)
        return jnp.sum(parts.astype(F32), axis=0)

    def scatter_plane(parts):
        d_here = lax.axis_index("dp")
        keep = lax.dynamic_index_in_dim(parts, d_here, 0, keepdims=False)
        away = lax.dynamic_index_in_dim(parts, 1 - d_here, 0, keepdims=False)
        return scatter_ctx(keep.astype(F32) + swap_dp(away.astype(BF16)).astype(F32))

    def per_device(
        tokens, qkv_weight, out_weight, norm1_gain, norm1_shift, norm2_gain, norm2_shift,
        inner_weight, outer_weight, router_weight, expert_inner, expert_outer,
        segments, routes, priority, cotangent,
    ):
        rows, width = tokens.shape[1:]
        length = segments.shape[1]
        rw = qkv_weight.shape[0]
        ff_rows = outer_weight.shape[0]
        nplane = nd * nc
        e_here = lax.axis_index("exp")
        group = width // nc

        x_low = to_seq(tokens[0])
        ints = jnp.concatenate([segments[0], routes[0, :, 0], priority[0, 0]])
        ints = to_seq(ints.reshape(-1, 128)).reshape(-1)
        segs, route, order = ints[:length], ints[length : length + rows], ints[length + rows :]

        small = jnp.concatenate(
            [norm1_gain, norm1_shift, norm2_gain, norm2_shift, router_weight.reshape(-1)]
        )
        small = lax.all_to_all(
            jnp.broadcast_to(small[None], (ndev,) + small.shape), AXES, 0, 0, tiled=True
        )
        gain1, shift1, gain2, shift2 = (
            small[:, i * rw : (i + 1) * rw].reshape(width).astype(F32) for i in range(4)
        )
        router = small[:, 4 * rw :].reshape(width, ne)

        ff = nplane * ff_rows
        qkv_part = jnp.moveaxis(qkv_weight.reshape(rw, 3, nc, group), 2, 0)
        qkv_part = jnp.tile(qkv_part.reshape(nc, rw, 3 * group), (ne // nc, 1, 1))
        inner_part = jnp.moveaxis(inner_weight.reshape(rw, nplane, ne, ff_rows), 2, 0)
        columns = jnp.concatenate([qkv_part, inner_part.reshape(ne, rw, ff)], axis=2)
        columns = lax.all_to_all(columns, "exp", 0, 0, tiled=True).reshape(ne * rw, -1)
        out_part = jnp.concatenate(jnp.split(out_weight, nc, axis=1), axis=0)
        out_part = jnp.pad(out_part, ((0, ne * rw - nc * rw), (0, 0)))
        bundle = gather_plane(jnp.concatenate([columns[:, : 3 * group], out_part], axis=1))
        w_qkv = bundle[..., : 3 * group].reshape(width, 3 * group)
        w_out = bundle[:, :, : nc * rw, 3 * group :].reshape(nplane, nc, rw, group)
        w_out = gather_exp(w_out, all_bits)
        w_out = jnp.transpose(w_out, (1, 0, 3, 2, 4)).reshape(width, width)
        inner_flat = columns[:, 3 * group :].reshape(-1, width)
        bundle = gather_plane(jnp.concatenate([inner_flat, outer_weight]))
        w_inner = bundle[:, :, : inner_flat.shape[0]].reshape(width, ff)
        w_outer = bundle[:, :, inner_flat.shape[0] :].reshape(ff, width)

        e_in_own, e_out_own = expert_inner[0], expert_outer[0]
        lanes = jnp.pad(router, ((0, 0), (0, 128 - ne)))
        e_in = jnp.concatenate([e_in_own, swap_dp(e_in_own), lanes], axis=1)
        e_out = jnp.concatenate([e_out_own, swap_dp(e_out_own)], axis=0)

        x = x_low.astype(F32)
        unit1, scale1 = norm_parts(x)
        normed = (unit1 * gain1 + shift1).astype(BF16)
        normed_all = gather_exp(normed, low_bits).reshape(length, width)
        qkv = dot(normed_all, w_qkv).astype(BF16)
        mixed = attention_fwd(qkv, segs, rows)
        attended = trade_exp(mixed.reshape(nc, rows, group), low_bits)
        attended = jnp.moveaxis(attended, 0, 1).reshape(rows, width)
        residual = x + dot(attended, w_out)
        unit2, scale2 = norm_parts(residual)
        normed2 = (unit2 * gain2 + shift2).astype(BF16)

        cot_low = to_seq(cotangent[0])
        cot = cot_low.astype(F32)
        capacity = (9 * rows + 8 * ne - 1) // (8 * ne)
        same = route[:, None] == route[None, :]
        earlier = order[None, :] < order[:, None]
        slot = jnp.sum(jnp.logical_and(same, earlier).astype(jnp.int32), axis=1)
        place = jnp.where(slot < capacity, (route ^ e_here) * capacity + slot, -1)
        slots = ne * capacity
        table = (jnp.arange(slots, dtype=jnp.int32)[:, None] == place[None, :]).astype(BF16)

        def to_experts(v):
            out = dot(table, v).astype(BF16).reshape(ne, capacity, width)
            out = trade_exp_rel(out, all_bits).reshape(slots, width)
            return gather_ctx(out).reshape(nc * slots, width)

        def from_experts(v):
            back = scatter_ctx(v.reshape(nc, slots, width)).astype(BF16)
            back = trade_exp_rel(back.reshape(ne, capacity, width), all_bits)
            return dot_tn(table, back.reshape(slots, width))

        e_cot = to_experts(cot_low)
        e_x = to_experts(normed2)

        cot_all = gather_exp_rel(cot_low, all_bits).reshape(ne * rows, width)
        n2_all = gather_exp_rel(normed2, all_bits).reshape(ne * rows, width)
        act, slope = gelu_pair(dot(n2_all, w_inner))
        act = act.astype(BF16)
        d_hidden = (dot_nt(cot_all, w_outer) * slope).astype(BF16)
        dense_part = dot(act, w_outer).reshape(ne, rows, width)
        d_n2_part = dot_nt(d_hidden, w_inner).reshape(ne, rows, width)
        both = scatter_exp_rel(jnp.stack([dense_part, d_n2_part], 1), all_bits)
        dense, d_n2_dense = both[0], both[1]
        d_outer = dot_tn(act, cot_all)
        d_inner = dot_tn(n2_all, d_hidden)

        mine = (jnp.arange(128, dtype=jnp.int32) == e_here).astype(F32)[None, :]
        e_result, d_e_x, own_in, other_in, own_out, other_out, d_router = expert_block(
            e_x, e_cot, e_in, e_out, mine, nc * slots // 3, ne
        )
        d_router = d_router[:, :ne]
        g_e_in = own_in + swap_dp(other_in).astype(F32)
        g_e_out = own_out + swap_dp(other_out).astype(F32)

        d_n2 = d_n2_dense + from_experts(d_e_x)
        picked = from_experts(e_result)
        probs = softmax_rows(dot(normed2, router))
        chosen = (route[:, None] == jnp.arange(ne, dtype=jnp.int32)[None, :]).astype(F32)
        gate = jnp.sum(probs * chosen, axis=1, keepdims=True)
        output = from_seq((residual + dense + gate * picked).astype(BF16))

        d_gain2 = jnp.sum(d_n2 * unit2, axis=0)
        d_shift2 = jnp.sum(d_n2, axis=0)
        d_residual = cot + norm_back(d_n2, unit2, scale2, gain2)
        d_branch = d_residual.astype(BF16)
        d_out = dot_tn(attended, d_branch)
        d_att = dot_nt(d_branch, w_out).astype(BF16)
        d_att = jnp.moveaxis(d_att.reshape(rows, nc, group), 1, 0)
        d_mixed = trade_exp(d_att, low_bits).reshape(length, group)
        d_qkv = jnp.concatenate(attention_bwd(qkv, d_mixed, segs, rows), axis=1)
        d_normed = dot_nt(d_qkv, w_qkv).reshape(nc, rows, width)
        d_normed = scatter_exp(d_normed, low_bits)
        d_w_qkv = dot_tn(normed_all, d_qkv)
        d_gain1 = jnp.sum(d_normed * unit1, axis=0)
        d_shift1 = jnp.sum(d_normed, axis=0)
        d_tokens = d_residual + norm_back(d_normed, unit1, scale1, gain1)
        d_tokens = from_seq(d_tokens.astype(BF16)).astype(F32)

        bundle = jnp.concatenate(
            [d_inner.reshape(nd, nc, -1, width), d_outer.reshape(nd, nc, -1, width)], axis=2
        )
        bundle = scatter_plane(bundle)
        g_outer = bundle[inner_flat.shape[0] :]
        g_inner = bundle[: inner_flat.shape[0]].reshape(ne, rw, ff)

        d_out = jnp.moveaxis(d_out.reshape(nplane, ne, rw, width), 1, 0)
        d_out = scatter_exp(d_out, all_bits).reshape(nd, nc, rw, nc, group)
        d_out = jnp.moveaxis(d_out, 3, 2).reshape(nd, nc, nc * rw, group)
        d_out = jnp.pad(d_out, ((0, 0), (0, 0), (0, ne * rw - nc * rw), (0, 0)))
        bundle = jnp.concatenate([d_w_qkv.reshape(nd, nc, ne * rw, -1), d_out], axis=3)
        bundle = scatter_plane(bundle)
        g_out = bundle[: nc * rw, 3 * group :].reshape(nc, rw, group)
        g_out = jnp.moveaxis(g_out, 0, 1).reshape(rw, width)
        g_qkv = bundle[:, : 3 * group].reshape(ne, rw, 3 * group)
        columns = jnp.concatenate([g_qkv, g_inner], axis=2).astype(BF16)
        columns = lax.all_to_all(columns, "exp", 0, 0, tiled=True)
        g_inner = columns[:, :, 3 * group :].reshape(ne, rw, nplane, ff_rows)
        g_inner = jnp.transpose(g_inner, (1, 2, 0, 3)).reshape(rw, -1).astype(F32)
        g_qkv = columns[:, :, : 3 * group].reshape(ne // nc, nc, rw, 3, group)
        g_qkv = jnp.sum(g_qkv.astype(F32), axis=0)
        g_qkv = jnp.transpose(g_qkv, (1, 2, 0, 3)).reshape(rw, 3 * width)

        small = jnp.concatenate([jnp.stack([d_gain1, d_shift1, d_gain2, d_shift2], 1), d_router], 1)
        small = lax.all_to_all(small.reshape(ndev, -1), AXES, 0, 0, tiled=True)
        small = jnp.sum(small, axis=0).reshape(rw, 4 + ne)

        return (
            output[None], d_tokens[None], g_qkv, g_out,
            small[:, 0], small[:, 1], small[:, 2], small[:, 3],
            g_inner, g_outer, small[:, 4:], g_e_in[None], g_e_out[None],
        )

    rest = ("dp", "ctx", "exp")
    seq = P(("dp", "exp"), "ctx", None)
    in_specs = (
        seq, P(rest, None), P(rest, None), P(rest), P(rest), P(rest), P(rest),
        P(rest, None), P(rest, None), P(rest, None),
        P("exp", None, ("dp", "ctx")), P("exp", ("dp", "ctx"), None),
        P(("dp", "exp"), None), seq, seq, seq,
    )
    out_specs = (
        seq, seq, P(rest, None), P(rest, None), P(rest), P(rest), P(rest), P(rest),
        P(rest, None), P(rest, None), P(rest, None),
        P("exp", None, ("dp", "ctx")), P("exp", ("dp", "ctx"), None),
    )
    return jax.shard_map(
        per_device, mesh=mesh, in_specs=in_specs, out_specs=out_specs, check_vma=False
    )
```

```python
import functools
import math

import jax
import jax.numpy as jnp
from jax import lax
from jax.experimental import pallas as pl
from jax.experimental.pallas import tpu as pltpu
from jax.sharding import PartitionSpec as P

HEADS = 16
HEAD_DIM = 64
AXES = ("dp", "ctx", "exp")
EPS = 1e-05
NEG = -1e30
GELU_A = 0.7978845608028654
GELU_B = 0.044715
SPREAD = 10
F32 = jnp.float32
BF16 = jnp.bfloat16


def dot(a, b):
    return jnp.dot(a, b, preferred_element_type=F32)


def dot_nt(a, b):
    return lax.dot_general(a, b, (((1,), (1,)), ((), ())), preferred_element_type=F32)


def dot_tn(a, b):
    return lax.dot_general(a, b, (((0,), (0,)), ((), ())), preferred_element_type=F32)


def norm_parts(z):
    average = jnp.mean(z, axis=-1, keepdims=True)
    centred = z - average
    scale = lax.rsqrt(jnp.mean(centred * centred, axis=-1, keepdims=True) + EPS)
    return centred * scale, scale


def norm_back(grad, unit, scale, gain):
    w = grad * gain
    return scale * (
        w
        - jnp.mean(w, axis=-1, keepdims=True)
        - unit * jnp.mean(w * unit, axis=-1, keepdims=True)
    )


def gelu_pair(u):
    square = u * u
    t = jnp.tanh(u * (GELU_A + GELU_A * GELU_B * square))
    half = 0.5 * (1.0 + t)
    return u * half, half + 0.5 * u * (1.0 - t * t) * (GELU_A + 3.0 * GELU_A * GELU_B * square)


def softmax_rows(v):
    raised = jnp.exp(v - jnp.max(v, axis=-1, keepdims=True))
    return raised / jnp.sum(raised, axis=-1, keepdims=True)


def assemble(full_ref, own, other, here):
    half = full_ref.shape[0] // 2
    full_ref[pl.ds(pl.multiple_of(here * half, half), half), :] = own
    full_ref[pl.ds(pl.multiple_of((1 - here) * half, half), half), :] = other


def assemble_attention(n, own_ref, other_ref, w_ref, wo_ref, here):
    planes, rows, width = own_ref.shape
    group = width // n
    small = wo_ref.shape[0] // (2 * planes)
    for ref, d in ((own_ref, here), (other_ref, 1 - here)):
        for c in range(planes):
            at = pl.multiple_of((d * planes + c) * rows, rows)
            w_ref[pl.ds(at, rows), :] = ref[c, :, : 3 * group]
            at = pl.multiple_of((d * planes + c) * small, small)
            for g in range(n):
                wo_ref[pl.ds(at, small), g * group : (g + 1) * group] = ref[
                    c, g * small : (g + 1) * small, 3 * group :
                ]


def attention_fwd_kernel(n, where_ref, *refs):
    xs, refs = refs[:n], refs[n:]
    own_ref, other_ref, segrow_ref, segcol_ref = refs[:4]
    qkv_ref, att_ref, keep_ref, away_ref, w_ref, wo_ref = refs[4:]
    block = xs[0].shape[0]
    group = att_ref.shape[1]
    pair = 2 * HEAD_DIM
    low, here = where_ref[0], where_ref[1]
    scale = 1.0 / math.sqrt(HEAD_DIM)
    assemble_attention(n, own_ref, other_ref, w_ref, wo_ref, here)

    def natural(i):
        return pl.ds(pl.multiple_of((low ^ i) * block, block), block)

    for i in range(n):
        qkv_ref[natural(i), :] = dot(xs[i][...], w_ref[...]).astype(BF16)

    first = lax.broadcasted_iota(jnp.int32, (block, pair), 1) < HEAD_DIM

    @pl.loop(0, group // pair)
    def _(p):
        lanes = [pl.ds(pl.multiple_of(j * group + p * pair, pair), pair) for j in range(3)]
        for i in range(n):
            ext = (i + 1) * block
            rows = pl.ds(i * block, block)
            q = qkv_ref[rows, lanes[0]] * jnp.asarray(scale, BF16)
            k = qkv_ref[pl.ds(0, ext), lanes[1]]
            v = qkv_ref[pl.ds(0, ext), lanes[2]]
            qpos = lax.broadcasted_iota(jnp.int32, (block, ext), 0) + i * block
            kpos = lax.broadcasted_iota(jnp.int32, (block, ext), 1)
            visible = jnp.logical_and(
                kpos <= qpos, segcol_ref[rows, :] == segrow_ref[:, pl.ds(0, ext)]
            )
            outs = []
            for half in range(2):
                mine = first if half == 0 else jnp.logical_not(first)
                s = jnp.where(visible, dot_nt(jnp.where(mine, q, jnp.zeros_like(q)), k), NEG)
                e = jnp.exp(s - jnp.max(s, axis=1, keepdims=True))
                outs.append(dot(e.astype(BF16), v) / jnp.sum(e, axis=1, keepdims=True))
            att_ref[rows, lanes[0]] = jnp.where(first, outs[0], outs[1]).astype(BF16)

    for i in range(n):
        part = dot(att_ref[natural(i), :], wo_ref[...]).astype(BF16)
        (away_ref if i % 2 else keep_ref)[i // 2] = part


def attention_bwd_kernel(n, where_ref, *refs):
    ds_in, xs, refs = refs[:n], refs[n : 2 * n], refs[2 * n :]
    own_ref, other_ref, segrow_ref, segcol_ref, qkv_ref, att_ref = refs[:6]
    keep_ref, away_ref, gown_ref, gother_ref = refs[6:10]
    w_ref, wo_ref, x_ref, db_ref, do_ref, dqkv_ref, dk_acc, dv_acc = refs[10:]
    block = xs[0].shape[0]
    length, group = att_ref.shape
    width = x_ref.shape[1]
    planes, wrows = own_ref.shape[:2]
    small = group // (2 * planes)
    pair = 2 * HEAD_DIM
    low, here = where_ref[0], where_ref[1]
    scale = 1.0 / math.sqrt(HEAD_DIM)
    assemble_attention(n, own_ref, other_ref, w_ref, wo_ref, here)

    def natural(i):
        return pl.ds(pl.multiple_of((low ^ i) * block, block), block)

    for i in range(n):
        x_ref[natural(i), :] = xs[i][...]
        db_ref[natural(i), :] = ds_in[i][...]
        do_ref[natural(i), :] = dot_nt(ds_in[i][...], wo_ref[...]).astype(BF16)

    first = lax.broadcasted_iota(jnp.int32, (block, pair), 1) < HEAD_DIM

    @pl.loop(0, group // pair)
    def _(p):
        lanes = [pl.ds(pl.multiple_of(j * group + p * pair, pair), pair) for j in range(3)]
        dk_acc[...] = jnp.zeros_like(dk_acc)
        dv_acc[...] = jnp.zeros_like(dv_acc)
        for i in range(n):
            ext = (i + 1) * block
            rows = pl.ds(i * block, block)
            keys = pl.ds(0, ext)
            q = qkv_ref[rows, lanes[0]] * jnp.asarray(scale, BF16)
            do = do_ref[rows, lanes[0]]
            k = qkv_ref[keys, lanes[1]]
            v = qkv_ref[keys, lanes[2]]
            qpos = lax.broadcasted_iota(jnp.int32, (ext, block), 1) + i * block
            kpos = lax.broadcasted_iota(jnp.int32, (ext, block), 0)
            visible = jnp.logical_and(kpos <= qpos, segcol_ref[keys, :] == segrow_ref[:, rows])
            dq = []
            for half in range(2):
                mine = first if half == 0 else jnp.logical_not(first)
                qh = jnp.where(mine, q, jnp.zeros_like(q))
                doh = jnp.where(mine, do, jnp.zeros_like(do))
                s = jnp.where(visible, dot_nt(k, qh), NEG)
                e = jnp.exp(s - jnp.max(s, axis=0, keepdims=True))
                e = e * (1.0 / jnp.sum(e, axis=0, keepdims=True))
                dp = dot_nt(v, doh)
                delta = jnp.sum(e * dp, axis=0, keepdims=True)
                ds = (e * (dp - delta)).astype(BF16)
                dv_acc[keys, :] += dot(e.astype(BF16), doh)
                dk_acc[keys, :] += dot(ds, qh)
                dq.append(dot_tn(ds, k))
            dqkv_ref[rows, lanes[0]] = (jnp.where(first, dq[0], dq[1]) * scale).astype(BF16)
        dqkv_ref[:, lanes[1]] = dk_acc[...].astype(BF16)
        dqkv_ref[:, lanes[2]] = dv_acc[...].astype(BF16)

    for i in range(n):
        part = dot_nt(dqkv_ref[natural(i), :], w_ref[...]).astype(BF16)
        (away_ref if i % 2 else keep_ref)[i // 2] = part
    wo_ref[...] = dot_tn(att_ref[...], db_ref[...]).astype(BF16)
    for ref, d in ((gown_ref, here), (gother_ref, 1 - here)):
        at = pl.ds(pl.multiple_of(d * (width // 2), width // 2), width // 2)
        grad = dot_tn(x_ref[:, at], dqkv_ref[...]).astype(BF16)
        for c in range(planes):
            ref[c, :, : 3 * group] = grad[c * wrows : (c + 1) * wrows]
            at = pl.multiple_of((d * planes + c) * small, small)
            for g in range(n):
                ref[c, g * small : (g + 1) * small, 3 * group :] = wo_ref[
                    pl.ds(at, small), g * group : (g + 1) * group
                ]


def vmem_call(kernel, out_shape, scratch, flops, transcendentals, where, *args):
    bytes_of = lambda a: math.prod(a.shape) * a.dtype.itemsize
    vmem = pl.BlockSpec(memory_space=pltpu.VMEM)
    return pl.pallas_call(
        kernel,
        in_specs=[pl.BlockSpec(memory_space=pltpu.SMEM)] + [vmem] * len(args),
        out_specs=[vmem] * len(out_shape),
        out_shape=out_shape,
        scratch_shapes=scratch,
        compiler_params=pltpu.CompilerParams(vmem_limit_bytes=60 * 1024 * 1024),
        cost_estimate=pl.CostEstimate(
            flops=SPREAD * flops,
            bytes_accessed=sum(map(bytes_of, args)) + sum(map(bytes_of, out_shape)),
            transcendentals=transcendentals,
        ),
    )(where, *args)


def shape16(*dims):
    return jax.ShapeDtypeStruct(dims, BF16)


def attention_fwd(where, xs, own, other, segs):
    n, (block, width) = len(xs), xs[0].shape
    length, group = n * block, width // n
    return vmem_call(
        functools.partial(attention_fwd_kernel, n),
        [
            shape16(length, 3 * group), shape16(length, group),
            shape16(n // 2, block, width), shape16(n // 2, block, width),
        ],
        [pltpu.VMEM((width, 3 * group), BF16), pltpu.VMEM((group, width), BF16)],
        8 * length * width * group + 8 * length * length * group,
        length * length * group // HEAD_DIM // 2,
        where, *xs, own, other, segs[None, :], segs[:, None],
    )


def attention_bwd(where, d_branch, xs, own, other, segs, qkv, att):
    n, (block, width) = len(xs), xs[0].shape
    length, group = n * block, width // n
    return vmem_call(
        functools.partial(attention_bwd_kernel, n),
        [
            shape16(n // 2, block, width), shape16(n // 2, block, width),
            shape16(*own.shape), shape16(*own.shape),
        ],
        [
            pltpu.VMEM((width, 3 * group), BF16), pltpu.VMEM((group, width), BF16),
            pltpu.VMEM((length, width), BF16), pltpu.VMEM((length, width), BF16),
            pltpu.VMEM((length, group), BF16), pltpu.VMEM((length, 3 * group), BF16),
            pltpu.VMEM((length, 2 * HEAD_DIM), F32), pltpu.VMEM((length, 2 * HEAD_DIM), F32),
        ],
        16 * length * width * group + 20 * length * length * group,
        length * length * group // HEAD_DIM // 2,
        where, *d_branch, *xs, own, other, segs[None, :], segs[:, None], qkv, att,
    )


def dense_kernel(n, ff, where_ref, *refs):
    xs, gs, refs = refs[:n], refs[n : 2 * n], refs[2 * n :]
    own_ref, other_ref, keep_ref, away_ref, gown_ref, gother_ref = refs[:6]
    wi_ref, wo_ref, x_ref, g_ref, act_ref, dh_ref = refs[6:]
    rows, width = xs[0].shape
    planes = own_ref.shape[0]
    here = where_ref[1]
    inner, outer = width // (2 * planes), ff // (2 * planes)
    for ref, d in ((own_ref, here), (other_ref, 1 - here)):
        for c in range(planes):
            at = pl.multiple_of((d * planes + c) * inner, inner)
            for g in range(width // ff):
                wi_ref[pl.ds(at + g * (inner * ff // width), inner * ff // width), :] = ref[
                    c, : inner * ff // width, g * ff : (g + 1) * ff
                ]
            at = pl.multiple_of((d * planes + c) * outer, outer)
            wo_ref[pl.ds(at, outer), :] = ref[c, inner * ff // width :, :]
    for i in range(n):
        x_ref[pl.ds(i * rows, rows), :] = xs[i][...]
        g_ref[pl.ds(i * rows, rows), :] = gs[i][...]

    @pl.loop(0, n // 2)
    def _(t):
        for odd, out_ref in ((0, keep_ref), (1, away_ref)):
            r = pl.ds(pl.multiple_of((2 * t + odd) * rows, rows), rows)
            act, slope = gelu_pair(dot(x_ref[r, :], wi_ref[...]))
            act = act.astype(BF16)
            dh = (dot_nt(g_ref[r, :], wo_ref[...]) * slope).astype(BF16)
            act_ref[r, :] = act
            dh_ref[r, :] = dh
            out_ref[0, t] = dot(act, wo_ref[...]).astype(BF16)
            out_ref[1, t] = dot_nt(dh, wi_ref[...]).astype(BF16)

    small = inner * ff // width
    for ref, d in ((gother_ref, 1 - here), (gown_ref, here)):
        c = pl.ds(pl.multiple_of(d * (ff // 2), ff // 2), ff // 2)
        grad = dot_tn(act_ref[:, c], g_ref[...]).astype(BF16)
        ref[:, small:, :] = grad.reshape(planes, outer, width)
        c = pl.ds(pl.multiple_of(d * (width // 2), width // 2), width // 2)
        grad = dot_tn(x_ref[:, c], dh_ref[...]).astype(BF16).reshape(planes, inner, ff)
        for g in range(width // ff):
            ref[:, :small, g * ff : (g + 1) * ff] = grad[:, g * small : (g + 1) * small]


def dense_block(where, xs, gs, own, other, ff):
    n, (rows, width) = len(xs), xs[0].shape
    tokens = n * rows
    both = shape16(2, n // 2, rows, width)
    return vmem_call(
        functools.partial(dense_kernel, n, ff),
        [both, both, shape16(*own.shape), shape16(*own.shape)],
        [
            pltpu.VMEM((width, ff), BF16), pltpu.VMEM((ff, width), BF16),
            pltpu.VMEM((tokens, width), BF16), pltpu.VMEM((tokens, width), BF16),
            pltpu.VMEM((tokens, ff), BF16), pltpu.VMEM((tokens, ff), BF16),
        ],
        12 * tokens * width * ff, tokens * ff,
        where, *xs, *gs, own, other,
    )


def expert_kernel(rows, ne, where_ref, *refs):
    x_ref, c_ref, wi_own, wi_other, wo_own, wo_other, router_ref, mine_ref = refs[:8]
    y_ref, dx_ref, gi_own, gi_other, go_own, go_other, gr_ref = refs[8:15]
    wi_ref, wo_ref, g_ref, act_ref, dh_ref = refs[15:]
    width = x_ref.shape[1]
    ff = wo_ref.shape[0]
    half = ff // 2
    wi_ref[:, :half] = wi_own[...]
    wi_ref[:, half:ff] = wi_other[...]
    wi_ref[:, ff:] = router_ref[...]
    wo_ref[:half, :] = wo_own[...]
    wo_ref[half:, :] = wo_other[...]
    mine = mine_ref[...]
    lanes = lax.broadcasted_iota(jnp.int32, (rows, mine.shape[1]), 1)

    @pl.loop(0, x_ref.shape[0] // rows)
    def _(t):
        r = pl.ds(pl.multiple_of(t * rows, rows), rows)
        hidden = dot(x_ref[r, :], wi_ref[...])
        logits = jnp.where(lanes < ne, hidden[:, ff:], NEG)
        raised = jnp.exp(logits - jnp.max(logits, axis=1, keepdims=True))
        probs = raised / jnp.sum(raised, axis=1, keepdims=True)
        gate = jnp.sum(probs * mine, axis=1, keepdims=True)
        act, slope = gelu_pair(hidden[:, :ff])
        act = act.astype(BF16)
        cot = c_ref[r, :].astype(F32)
        grad = (gate * cot).astype(BF16)
        dh = (dot_nt(grad, wo_ref[...]) * slope).astype(BF16)
        result = dot(act, wo_ref[...])
        d_gate = jnp.sum(cot * result, axis=1, keepdims=True)
        act_ref[r, :] = act
        g_ref[r, :] = grad
        dh_ref[r, :ff] = dh
        dh_ref[r, ff:] = (d_gate * probs * (mine - gate)).astype(BF16)
        y_ref[r, :] = result.astype(BF16)
        dx_ref[r, :] = dot_nt(dh_ref[r, :], wi_ref[...]).astype(BF16)

    go_other[...] = dot_tn(act_ref[:, half:], g_ref[...]).astype(BF16)
    go_own[...] = dot_tn(act_ref[:, :half], g_ref[...]).astype(BF16)
    for j in range(2):
        c = pl.ds(j * (width // 2), width // 2)
        grad = dot_tn(x_ref[:, c], dh_ref[...])
        gi_own[c, :] = grad[:, :half].astype(BF16)
        gi_other[c, :] = grad[:, half:ff].astype(BF16)
        gr_ref[c, :] = grad[:, ff:]


def expert_block(where, x, cot, wi_own, wi_other, wo_own, wo_other, router, mine, rows, ne):
    tokens, width = x.shape
    ff, pad = 2 * wo_own.shape[0], router.shape[1]
    return vmem_call(
        functools.partial(expert_kernel, rows, ne),
        [shape16(tokens, width)] * 2
        + [shape16(*w.shape) for w in (wi_own, wi_other, wo_own, wo_other)]
        + [jax.ShapeDtypeStruct((width, pad), F32)],
        [
            pltpu.VMEM((width, ff + pad), BF16), pltpu.VMEM((ff, width), BF16),
            pltpu.VMEM((tokens, width), BF16),
            pltpu.VMEM((tokens, ff), BF16), pltpu.VMEM((tokens, ff + pad), BF16),
        ],
        12 * tokens * width * ff, tokens * ff,
        where, x, cot, wi_own, wi_other, wo_own, wo_other, router, mine,
    )


def solution(mesh):
    nd, nc, ne = (mesh.shape[a] for a in AXES)
    ndev = nd * nc * ne
    bits_of = lambda n: [1 << b for b in range(n.bit_length() - 1)]
    low_bits, all_bits = bits_of(nc), bits_of(ne)
    high_bits = [b for b in all_bits if b not in low_bits]
    nh = ne // nc


    def send(x, target):
        pairs = []
        for d in range(nd):
            for c in range(nc):
                for e in range(ne):
                    to = target(d, c, e)
                    if to is not None:
                        pairs.append(((d * nc + c) * ne + e, (to[0] * nc + to[1]) * ne + to[2]))
        return lax.ppermute(x, AXES, pairs)

    def swap_exp(x, bit):
        return send(x, lambda d, c, e: (d, c, e ^ bit))

    def swap_dp(x):
        return send(x, lambda d, c, e: (d ^ 1, c, e))

    def reverse(i):
        return int(format(i, "b").zfill(len(low_bits))[::-1], 2)

    def to_seq(x):
        return send(x, lambda d, c, e: (d, reverse(e % nc), e - e % nc + c))

    def from_seq(x):
        return send(x, lambda d, c, e: (d, e % nc, e - e % nc + reverse(c)))

    def to_seq_by(x, *others):
        x = after(swap_exp(x, nc // 2), *others)
        return send(x, lambda d, c, e: (d, reverse((e ^ (nc // 2)) % nc), e - e % nc + c))

    def from_seq_by(x):
        x = send(x, lambda d, c, e: (d, e % nc, (e - e % nc + reverse(c)) ^ (nc // 2)))
        return swap_exp(x, nc // 2)

    def after(x, *others):
        return lax.optimization_barrier((x,) + others)[0]

    def my_bit(bit):
        return (lax.axis_index("exp") // bit) % 2

    def ordered(mine, other, index, axis):
        return jnp.where(
            index == 0, jnp.stack([mine, other], axis), jnp.stack([other, mine], axis)
        )

    def gather_exp(x, bits):
        out = x[None]
        for bit in reversed(bits):
            out = ordered(out, swap_exp(out, bit), my_bit(bit), 1)
            out = out.reshape((-1,) + x.shape)
        return out

    def pieces_exp(x, bits):
        out = [x]
        for bit in reversed(bits):
            out = [v for own in out for v in (own, swap_exp(own, bit))]
        return out

    def scatter_exp_rel(keep, away, bits):
        parts = keep.astype(F32) + swap_exp(away, bits[0]).astype(F32)
        for bit in bits[1:]:
            pairs = parts.reshape((parts.shape[0], -1, 2) + parts.shape[2:])
            away = swap_exp(pairs[:, :, 1].astype(BF16), bit)
            parts = pairs[:, :, 0].astype(F32) + away.astype(F32)
        return parts[:, 0], away

    def split_bit(x, position, count):
        shape = x.shape
        return x.reshape((shape[0] >> (position + 1), 2, 1 << position) + shape[1:])

    def scatter_exp(parts, bits):
        for bit in bits:
            pairs = parts.reshape((-1, 2) + parts.shape[1:])
            mine = my_bit(bit)
            keep = lax.dynamic_index_in_dim(pairs, mine, 1, keepdims=False)
            away = lax.dynamic_index_in_dim(pairs, 1 - mine, 1, keepdims=False)
            parts = keep.astype(F32) + swap_exp(away.astype(BF16), bit).astype(F32)
        return parts[0]

    def trade_exp(parts, bits):
        for position, bit in enumerate(bits):
            pairs = split_bit(parts, position, len(bits))
            mine = my_bit(bit)
            keep = lax.dynamic_index_in_dim(pairs, mine, 1, keepdims=False)
            away = lax.dynamic_index_in_dim(pairs, 1 - mine, 1, keepdims=False)
            parts = ordered(keep, swap_exp(away, bit), mine, 1).reshape(parts.shape)
        return parts

    def gather_ctx(x):
        return lax.all_to_all(
            jnp.broadcast_to(x[None], (nc,) + x.shape), "ctx", 0, 0, tiled=True
        )

    def scatter_ctx(parts):
        parts = lax.all_to_all(parts.astype(BF16), "ctx", 0, 0, tiled=True)
        return jnp.sum(parts.astype(F32), axis=0)

    def scatter_plane(own, other, *others):
        both = (own.astype(F32) + other.astype(F32)).astype(BF16)
        return scatter_ctx(after(both, *others))

    def out_place(d, c, e):
        low, rest = divmod((d * nc + c) * ne + e, ndev // nc)
        return rest // (nc * nh), rest // nh % nc, rest % nh * nc + low

    def out_to(x):
        return send(x, out_place)

    def out_from(x):
        back = {
            out_place(d, c, e): (d, c, e) for d in range(nd) for c in range(nc) for e in range(ne)
        }
        return send(x, lambda d, c, e: back[(d, c, e)])

    def per_device(
        tokens, qkv_weight, out_weight, norm1_gain, norm1_shift, norm2_gain, norm2_shift,
        inner_weight, outer_weight, router_weight, expert_inner, expert_outer,
        segments, routes, priority, cotangent,
    ):
        rows, width = tokens.shape[1:]
        length = segments.shape[1]
        rw = qkv_weight.shape[0]
        ff_rows = outer_weight.shape[0]
        nplane = nd * nc
        e_here = lax.axis_index("exp")
        group = width // nc

        x_low = to_seq(tokens[0])
        capacity = (9 * rows + 8 * ne - 1) // (8 * ne)
        slots = ne * capacity
        route, order = routes[0, :, 0], priority[0, 0]
        same = route[:, None] == route[None, :]
        earlier = order[None, :] < order[:, None]
        slot = jnp.sum(jnp.logical_and(same, earlier).astype(jnp.int32), axis=1)
        place = jnp.where(slot < capacity, route * capacity + slot, -1)

        table_there = (jnp.arange(slots, dtype=jnp.int32)[:, None] == place[None, :]).astype(BF16)
        ints = jnp.concatenate([segments[0], route, place])
        ints = to_seq(ints.reshape(-1, 128)).reshape(-1)
        segs, route, place = ints[:length], ints[length : length + rows], ints[length + rows :]

        def table_of(place):
            return (jnp.arange(slots, dtype=jnp.int32)[:, None] == place[None, :]).astype(BF16)

        table = table_of(place)

        def rows_out(table, v):
            return dot(table, v).astype(BF16).reshape(ne, capacity, width)

        def to_experts(table, v):
            out = jnp.broadcast_to(rows_out(table, v)[None], (nc, ne, capacity, width))
            out = out.reshape(nc * ne, capacity, width)
            return lax.all_to_all(out, ("ctx", "exp"), 0, 0, tiled=True)

        def from_experts(v):
            back = v.reshape(nc * ne, capacity, width)
            back = lax.all_to_all(back, ("ctx", "exp"), 0, 0, tiled=True)
            return dot_tn(jnp.tile(table, (nc, 1)), back.reshape(nc * slots, width)), back

        small = jnp.concatenate(
            [norm1_gain, norm1_shift, norm2_gain, norm2_shift, router_weight.reshape(-1)]
        )
        small = lax.all_to_all(
            jnp.broadcast_to(small[None], (ndev,) + small.shape), AXES, 0, 0, tiled=True
        )
        ff = nplane * ff_rows
        where = jnp.stack([e_here % nc, lax.axis_index("dp")]).astype(jnp.int32)
        qkv_part = jnp.moveaxis(qkv_weight.reshape(rw, 3, nc, group), 2, 0)
        qkv_part = jnp.tile(qkv_part.reshape(nc, rw, 3 * group), (nh, 1, 1))
        inner_part = jnp.moveaxis(inner_weight.reshape(rw, nplane, ne, ff_rows), 2, 0)
        columns = jnp.concatenate([qkv_part, inner_part.reshape(ne, rw, ff)], axis=2)
        columns = lax.all_to_all(columns, "exp", 0, 0, tiled=True).reshape(ne * rw, -1)
        out_part = gather_exp(out_to(out_weight), high_bits).reshape(nh * rw, nc, group)
        out_part = jnp.swapaxes(out_part, 0, 1).reshape(ne * rw, group)
        bundle = jnp.concatenate([columns[:, : 3 * group], out_part], axis=1)
        cot_low = to_seq_by(cotangent[0])
        ei_other = swap_dp(expert_inner[0])
        att_own = gather_ctx(after(bundle, x_low, small, cot_low, ei_other))
        ei_own, eo_own = expert_inner[0], expert_outer[0]
        gain1, shift1, gain2, shift2 = (
            small[:, i * rw : (i + 1) * rw].reshape(width).astype(F32) for i in range(4)
        )
        router = small[:, 4 * rw :].reshape(width, ne)

        x = x_low.astype(F32)
        unit1, scale1 = norm_parts(x)
        normed = pieces_exp((unit1 * gain1 + shift1).astype(BF16), low_bits)
        att_other = swap_dp(att_own)
        eo_other = swap_dp(after(eo_own, att_other))
        qkv, attended, keep, away = attention_fwd(where, normed, att_own, att_other, segs)
        e_cot = trade_exp(rows_out(table_there, cotangent[0]), all_bits)
        part = columns[:, 3 * group :].reshape(width // ff, -1, ff)
        part = jnp.concatenate([jnp.swapaxes(part, 0, 1).reshape(-1, width), outer_weight])
        ff_own = gather_ctx(after(part, att_own, e_cot))
        ff_other = swap_dp(ff_own)
        keep = after(keep, ff_own)
        residual = x + scatter_exp_rel(keep[None], away[None], low_bits)[0][0]
        e_cot = gather_ctx(after(e_cot, ff_own, keep)).reshape(nc, nh, nc, capacity, width)
        cot_all = pieces_exp(cot_low, all_bits)
        residual = after(residual, eo_other, *cot_all)
        unit2, scale2 = norm_parts(residual)
        normed2 = (unit2 * gain2 + shift2).astype(BF16)

        cot = cot_low.astype(F32)
        e_cot = jnp.stack([e_cot[:, :, reverse(c)] for c in range(nc)])
        e_cot = jnp.moveaxis(e_cot, 1, 2).reshape(nc * slots, width)
        e_x = to_experts(table, normed2).reshape(nc * slots, width)
        n2_all = pieces_exp(normed2, all_bits)
        keep, away, ff_keep, ff_away = dense_block(where, n2_all, cot_all, ff_own, ff_other, ff)
        ff_away = swap_dp(ff_away)
        both, last = scatter_exp_rel(keep, away, all_bits)
        dense, d_n2_dense = both[0], both[1]

        e_x = after(e_x, keep)
        mine = (jnp.arange(128, dtype=jnp.int32) == e_here).astype(F32)[None, :]
        lanes = jnp.pad(router, ((0, 0), (0, 128 - ne)))
        e_result, d_e_x, gi_own, gi_other, go_own, go_other, d_router = expert_block(
            where, e_x, e_cot, ei_own, ei_other, eo_own, eo_other, lanes, mine,
            nc * slots // 4, ne,
        )
        d_router = d_router[:, :ne]
        gi_other, go_other = swap_dp(gi_other), swap_dp(go_other)

        d_e_x = after(d_e_x, ff_away, last)
        d_e_x, back = from_experts(d_e_x)
        d_n2 = d_n2_dense + d_e_x
        g_e_in = gi_own.astype(F32) + gi_other.astype(F32)
        g_e_out = go_own.astype(F32) + go_other.astype(F32)
        d_gain2 = jnp.sum(d_n2 * unit2, axis=0)
        d_shift2 = jnp.sum(d_n2, axis=0)
        d_residual = cot + norm_back(d_n2, unit2, scale2, gain2)
        d_branch = pieces_exp(d_residual.astype(BF16), low_bits)
        part = scatter_plane(ff_keep, ff_away, back, gi_other, go_other)
        e_result = scatter_ctx(after(e_result, part).reshape(nc, slots, width)).astype(BF16)
        picked = trade_exp(e_result.reshape(ne, capacity, width), all_bits)
        picked = dot_tn(table, picked.reshape(slots, width))
        probs = softmax_rows(dot(normed2, router))
        chosen = (route[:, None] == jnp.arange(ne, dtype=jnp.int32)[None, :]).astype(F32)
        gate = jnp.sum(probs * chosen, axis=1, keepdims=True)
        output = from_seq((residual + dense + gate * picked).astype(BF16))

        d_branch[0] = after(d_branch[0], part)
        keep, away, att_keep, att_away = attention_bwd(
            where, d_branch, normed, att_own, att_other, segs, qkv, attended
        )
        d_normed = scatter_exp_rel(keep[None], away[None], low_bits)[0][0]
        d_gain1 = jnp.sum(d_normed * unit1, axis=0)
        d_shift1 = jnp.sum(d_normed, axis=0)
        d_tokens = d_residual + norm_back(d_normed, unit1, scale1, gain1)
        d_tokens = from_seq(d_tokens.astype(BF16)).astype(F32)

        g_outer = part[width * ff // (nplane * width) :]
        g_inner = part[: width * ff // (nplane * width)].reshape(-1, width // ff, ff)
        g_inner = jnp.swapaxes(g_inner, 0, 1).reshape(ne, rw, ff)
        bundle = scatter_plane(att_keep, swap_dp(att_away), e_result)
        g_out = bundle[:, 3 * group :].reshape(nc, nh * rw, group)
        g_out = jnp.swapaxes(g_out, 0, 1).reshape(nh, rw, width)
        g_out = out_from(scatter_exp(g_out, high_bits).astype(BF16)).astype(F32)
        g_qkv = bundle[:, : 3 * group].reshape(ne, rw, 3 * group)
        columns = jnp.concatenate([g_qkv, g_inner], axis=2).astype(BF16)
        columns = lax.all_to_all(columns, "exp", 0, 0, tiled=True)
        g_inner = columns[:, :, 3 * group :].reshape(ne, rw, nplane, ff_rows)
        g_inner = jnp.transpose(g_inner, (1, 2, 0, 3)).reshape(rw, -1).astype(F32)
        g_qkv = columns[:, :, : 3 * group].reshape(nh, nc, rw, 3, group)
        g_qkv = jnp.sum(g_qkv.astype(F32), axis=0)
        g_qkv = jnp.transpose(g_qkv, (1, 2, 0, 3)).reshape(rw, 3 * width)

        small = jnp.concatenate([jnp.stack([d_gain1, d_shift1, d_gain2, d_shift2], 1), d_router], 1)
        small = after(small.reshape(ndev, -1), bundle)
        small = lax.all_to_all(small, AXES, 0, 0, tiled=True)
        small = jnp.sum(small, axis=0).reshape(rw, 4 + ne)

        return (
            output[None], d_tokens[None], g_qkv, g_out,
            small[:, 0], small[:, 1], small[:, 2], small[:, 3],
            g_inner, g_outer, small[:, 4:], g_e_in[None].astype(F32), g_e_out[None].astype(F32),
        )

    rest = ("dp", "ctx", "exp")
    seq = P(("dp", "exp"), "ctx", None)
    in_specs = (
        seq, P(rest, None), P(rest, None), P(rest), P(rest), P(rest), P(rest),
        P(rest, None), P(rest, None), P(rest, None),
        P("exp", None, ("dp", "ctx")), P("exp", ("dp", "ctx"), None),
        P(("dp", "exp"), None), seq, seq, seq,
    )
    out_specs = (
        seq, seq, P(rest, None), P(rest, None), P(rest), P(rest), P(rest), P(rest),
        P(rest, None), P(rest, None), P(rest, None),
        P("exp", None, ("dp", "ctx")), P("exp", ("dp", "ctx"), None),
    )
    return jax.shard_map(
        per_device, mesh=mesh, in_specs=in_specs, out_specs=out_specs, check_vma=False
    )
```

```python
import functools
import math

import jax
import jax.numpy as jnp
from jax import lax
from jax.experimental import pallas as pl
from jax.experimental.pallas import tpu as pltpu
from jax.sharding import PartitionSpec as P

HEADS = 16
HEAD_DIM = 64
AXES = ("dp", "ctx", "exp")
EPS = 1e-05
NEG = -1e30
GELU_A = 0.7978845608028654
GELU_B = 0.044715
SPREAD = 10
F32 = jnp.float32
BF16 = jnp.bfloat16


def dot(a, b):
    return jnp.dot(a, b, preferred_element_type=F32)


def dot_nt(a, b):
    return lax.dot_general(a, b, (((1,), (1,)), ((), ())), preferred_element_type=F32)


def dot_tn(a, b):
    return lax.dot_general(a, b, (((0,), (0,)), ((), ())), preferred_element_type=F32)


def norm_parts(z):
    average = jnp.mean(z, axis=-1, keepdims=True)
    centred = z - average
    scale = lax.rsqrt(jnp.mean(centred * centred, axis=-1, keepdims=True) + EPS)
    return centred * scale, scale


def norm_back(grad, unit, scale, gain):
    w = grad * gain
    return scale * (
        w
        - jnp.mean(w, axis=-1, keepdims=True)
        - unit * jnp.mean(w * unit, axis=-1, keepdims=True)
    )


def gelu_pair(u):
    square = u * u
    t = jnp.tanh(u * (GELU_A + GELU_A * GELU_B * square))
    half = 0.5 * (1.0 + t)
    return u * half, half + 0.5 * u * (1.0 - t * t) * (GELU_A + 3.0 * GELU_A * GELU_B * square)


def softmax_rows(v):
    raised = jnp.exp(v - jnp.max(v, axis=-1, keepdims=True))
    return raised / jnp.sum(raised, axis=-1, keepdims=True)


def assemble(full_ref, own, other, here):
    half = full_ref.shape[0] // 2
    full_ref[pl.ds(pl.multiple_of(here * half, half), half), :] = own
    full_ref[pl.ds(pl.multiple_of((1 - here) * half, half), half), :] = other


def assemble_attention(n, own_ref, other_ref, w_ref, wo_ref, here):
    planes, rows, width = own_ref.shape
    group = width // n
    small = wo_ref.shape[0] // (2 * planes)
    for ref, d in ((own_ref, here), (other_ref, 1 - here)):
        for c in range(planes):
            at = pl.multiple_of((d * planes + c) * rows, rows)
            w_ref[pl.ds(at, rows), :] = ref[c, :, : 3 * group]
            at = pl.multiple_of((d * planes + c) * small, small)
            for g in range(n):
                wo_ref[pl.ds(at, small), g * group : (g + 1) * group] = ref[
                    c, g * small : (g + 1) * small, 3 * group :
                ]


def attention_fwd_kernel(n, where_ref, *refs):
    xs, refs = refs[:n], refs[n:]
    own_ref, other_ref, segrow_ref, segcol_ref = refs[:4]
    qkv_ref, att_ref, keep_ref, away_ref, w_ref, wo_ref = refs[4:]
    block = xs[0].shape[0]
    group = att_ref.shape[1]
    pair = 2 * HEAD_DIM
    low, here = where_ref[0], where_ref[1]
    scale = 1.0 / math.sqrt(HEAD_DIM)
    assemble_attention(n, own_ref, other_ref, w_ref, wo_ref, here)

    def natural(i):
        return pl.ds(pl.multiple_of((low ^ i) * block, block), block)

    for i in range(n):
        qkv_ref[natural(i), :] = dot(xs[i][...], w_ref[...]).astype(BF16)

    first = lax.broadcasted_iota(jnp.int32, (block, pair), 1) < HEAD_DIM

    @pl.loop(0, group // pair)
    def _(p):
        lanes = [pl.ds(pl.multiple_of(j * group + p * pair, pair), pair) for j in range(3)]
        for i in range(n):
            ext = (i + 1) * block
            rows = pl.ds(i * block, block)
            q = qkv_ref[rows, lanes[0]] * jnp.asarray(scale, BF16)
            k = qkv_ref[pl.ds(0, ext), lanes[1]]
            v = qkv_ref[pl.ds(0, ext), lanes[2]]
            qpos = lax.broadcasted_iota(jnp.int32, (block, ext), 0) + i * block
            kpos = lax.broadcasted_iota(jnp.int32, (block, ext), 1)
            visible = jnp.logical_and(
                kpos <= qpos, segcol_ref[rows, :] == segrow_ref[:, pl.ds(0, ext)]
            )
            outs = []
            for half in range(2):
                mine = first if half == 0 else jnp.logical_not(first)
                s = jnp.where(visible, dot_nt(jnp.where(mine, q, jnp.zeros_like(q)), k), NEG)
                e = jnp.exp(s - jnp.max(s, axis=1, keepdims=True))
                outs.append(dot(e.astype(BF16), v) / jnp.sum(e, axis=1, keepdims=True))
            att_ref[rows, lanes[0]] = jnp.where(first, outs[0], outs[1]).astype(BF16)

    for i in range(n):
        part = dot(att_ref[natural(i), :], wo_ref[...]).astype(BF16)
        (away_ref if i % 2 else keep_ref)[i // 2] = part


def attention_bwd_kernel(n, where_ref, *refs):
    ds_in, xs, refs = refs[:n], refs[n : 2 * n], refs[2 * n :]
    own_ref, other_ref, segrow_ref, segcol_ref, qkv_ref, att_ref = refs[:6]
    keep_ref, away_ref, gown_ref, gother_ref = refs[6:10]
    w_ref, wo_ref, x_ref, db_ref, do_ref, dqkv_ref, dk_acc, dv_acc = refs[10:]
    block = xs[0].shape[0]
    length, group = att_ref.shape
    width = x_ref.shape[1]
    planes, wrows = own_ref.shape[:2]
    small = group // (2 * planes)
    pair = 2 * HEAD_DIM
    low, here = where_ref[0], where_ref[1]
    scale = 1.0 / math.sqrt(HEAD_DIM)
    assemble_attention(n, own_ref, other_ref, w_ref, wo_ref, here)

    def natural(i):
        return pl.ds(pl.multiple_of((low ^ i) * block, block), block)

    for i in range(n):
        x_ref[natural(i), :] = xs[i][...]
        db_ref[natural(i), :] = ds_in[i][...]
        do_ref[natural(i), :] = dot_nt(ds_in[i][...], wo_ref[...]).astype(BF16)

    first = lax.broadcasted_iota(jnp.int32, (block, pair), 1) < HEAD_DIM

    @pl.loop(0, group // pair)
    def _(p):
        lanes = [pl.ds(pl.multiple_of(j * group + p * pair, pair), pair) for j in range(3)]
        dk_acc[...] = jnp.zeros_like(dk_acc)
        dv_acc[...] = jnp.zeros_like(dv_acc)
        for i in range(n):
            ext = (i + 1) * block
            rows = pl.ds(i * block, block)
            keys = pl.ds(0, ext)
            q = qkv_ref[rows, lanes[0]] * jnp.asarray(scale, BF16)
            do = do_ref[rows, lanes[0]]
            k = qkv_ref[keys, lanes[1]]
            v = qkv_ref[keys, lanes[2]]
            qpos = lax.broadcasted_iota(jnp.int32, (ext, block), 1) + i * block
            kpos = lax.broadcasted_iota(jnp.int32, (ext, block), 0)
            visible = jnp.logical_and(kpos <= qpos, segcol_ref[keys, :] == segrow_ref[:, rows])
            dq = []
            for half in range(2):
                mine = first if half == 0 else jnp.logical_not(first)
                qh = jnp.where(mine, q, jnp.zeros_like(q))
                doh = jnp.where(mine, do, jnp.zeros_like(do))
                s = jnp.where(visible, dot_nt(k, qh), NEG)
                e = jnp.exp(s - jnp.max(s, axis=0, keepdims=True))
                e = e * (1.0 / jnp.sum(e, axis=0, keepdims=True))
                dp = dot_nt(v, doh)
                delta = jnp.sum(e * dp, axis=0, keepdims=True)
                ds = (e * (dp - delta)).astype(BF16)
                dv_acc[keys, :] += dot(e.astype(BF16), doh)
                dk_acc[keys, :] += dot(ds, qh)
                dq.append(dot_tn(ds, k))
            dqkv_ref[rows, lanes[0]] = (jnp.where(first, dq[0], dq[1]) * scale).astype(BF16)
        dqkv_ref[:, lanes[1]] = dk_acc[...].astype(BF16)
        dqkv_ref[:, lanes[2]] = dv_acc[...].astype(BF16)

    for i in range(n):
        part = dot_nt(dqkv_ref[natural(i), :], w_ref[...]).astype(BF16)
        (away_ref if i % 2 else keep_ref)[i // 2] = part
    wo_ref[...] = dot_tn(att_ref[...], db_ref[...]).astype(BF16)
    for ref, d in ((gown_ref, here), (gother_ref, 1 - here)):
        at = pl.ds(pl.multiple_of(d * (width // 2), width // 2), width // 2)
        grad = dot_tn(x_ref[:, at], dqkv_ref[...]).astype(BF16)
        for c in range(planes):
            ref[c, :, : 3 * group] = grad[c * wrows : (c + 1) * wrows]
            at = pl.multiple_of((d * planes + c) * small, small)
            for g in range(n):
                ref[c, g * small : (g + 1) * small, 3 * group :] = wo_ref[
                    pl.ds(at, small), g * group : (g + 1) * group
                ]


def vmem_call(kernel, out_shape, scratch, flops, transcendentals, where, *args):
    bytes_of = lambda a: math.prod(a.shape) * a.dtype.itemsize
    vmem = pl.BlockSpec(memory_space=pltpu.VMEM)
    return pl.pallas_call(
        kernel,
        in_specs=[pl.BlockSpec(memory_space=pltpu.SMEM)] + [vmem] * len(args),
        out_specs=[vmem] * len(out_shape),
        out_shape=out_shape,
        scratch_shapes=scratch,
        compiler_params=pltpu.CompilerParams(vmem_limit_bytes=60 * 1024 * 1024),
        cost_estimate=pl.CostEstimate(
            flops=SPREAD * flops,
            bytes_accessed=sum(map(bytes_of, args)) + sum(map(bytes_of, out_shape)),
            transcendentals=transcendentals,
        ),
    )(where, *args)


def shape16(*dims):
    return jax.ShapeDtypeStruct(dims, BF16)


def attention_fwd(where, xs, own, other, segs):
    n, (block, width) = len(xs), xs[0].shape
    length, group = n * block, width // n
    return vmem_call(
        functools.partial(attention_fwd_kernel, n),
        [
            shape16(length, 3 * group), shape16(length, group),
            shape16(n // 2, block, width), shape16(n // 2, block, width),
        ],
        [pltpu.VMEM((width, 3 * group), BF16), pltpu.VMEM((group, width), BF16)],
        8 * length * width * group + 8 * length * length * group,
        length * length * group // HEAD_DIM // 2,
        where, *xs, own, other, segs[None, :], segs[:, None],
    )


def attention_bwd(where, d_branch, xs, own, other, segs, qkv, att):
    n, (block, width) = len(xs), xs[0].shape
    length, group = n * block, width // n
    return vmem_call(
        functools.partial(attention_bwd_kernel, n),
        [
            shape16(n // 2, block, width), shape16(n // 2, block, width),
            shape16(*own.shape), shape16(*own.shape),
        ],
        [
            pltpu.VMEM((width, 3 * group), BF16), pltpu.VMEM((group, width), BF16),
            pltpu.VMEM((length, width), BF16), pltpu.VMEM((length, width), BF16),
            pltpu.VMEM((length, group), BF16), pltpu.VMEM((length, 3 * group), BF16),
            pltpu.VMEM((length, 2 * HEAD_DIM), F32), pltpu.VMEM((length, 2 * HEAD_DIM), F32),
        ],
        16 * length * width * group + 20 * length * length * group,
        length * length * group // HEAD_DIM // 2,
        where, *d_branch, *xs, own, other, segs[None, :], segs[:, None], qkv, att,
    )


def dense_kernel(n, ff, where_ref, *refs):
    xs, gs, refs = refs[:n], refs[n : 2 * n], refs[2 * n :]
    own_ref, other_ref, keep_ref, away_ref, gown_ref, gother_ref = refs[:6]
    wi_ref, wo_ref, x_ref, g_ref, act_ref, dh_ref = refs[6:]
    rows, width = xs[0].shape
    planes = own_ref.shape[0]
    here = where_ref[1]
    inner, outer = width // (2 * planes), ff // (2 * planes)
    for ref, d in ((own_ref, here), (other_ref, 1 - here)):
        for c in range(planes):
            at = pl.multiple_of((d * planes + c) * inner, inner)
            for g in range(width // ff):
                wi_ref[pl.ds(at + g * (inner * ff // width), inner * ff // width), :] = ref[
                    c, : inner * ff // width, g * ff : (g + 1) * ff
                ]
            at = pl.multiple_of((d * planes + c) * outer, outer)
            wo_ref[pl.ds(at, outer), :] = ref[c, inner * ff // width :, :]
    for i in range(n):
        x_ref[pl.ds(i * rows, rows), :] = xs[i][...]
        g_ref[pl.ds(i * rows, rows), :] = gs[i][...]

    @pl.loop(0, n // 2)
    def _(t):
        for odd, out_ref in ((0, keep_ref), (1, away_ref)):
            r = pl.ds(pl.multiple_of((2 * t + odd) * rows, rows), rows)
            act, slope = gelu_pair(dot(x_ref[r, :], wi_ref[...]))
            act = act.astype(BF16)
            dh = (dot_nt(g_ref[r, :], wo_ref[...]) * slope).astype(BF16)
            act_ref[r, :] = act
            dh_ref[r, :] = dh
            out_ref[0, t] = dot(act, wo_ref[...]).astype(BF16)
            out_ref[1, t] = dot_nt(dh, wi_ref[...]).astype(BF16)

    small = inner * ff // width
    for ref, d in ((gother_ref, 1 - here), (gown_ref, here)):
        c = pl.ds(pl.multiple_of(d * (ff // 2), ff // 2), ff // 2)
        grad = dot_tn(act_ref[:, c], g_ref[...]).astype(BF16)
        ref[:, small:, :] = grad.reshape(planes, outer, width)
        c = pl.ds(pl.multiple_of(d * (width // 2), width // 2), width // 2)
        grad = dot_tn(x_ref[:, c], dh_ref[...]).astype(BF16).reshape(planes, inner, ff)
        for g in range(width // ff):
            ref[:, :small, g * ff : (g + 1) * ff] = grad[:, g * small : (g + 1) * small]


def dense_block(where, xs, gs, own, other, ff):
    n, (rows, width) = len(xs), xs[0].shape
    tokens = n * rows
    both = shape16(2, n // 2, rows, width)
    return vmem_call(
        functools.partial(dense_kernel, n, ff),
        [both, both, shape16(*own.shape), shape16(*own.shape)],
        [
            pltpu.VMEM((width, ff), BF16), pltpu.VMEM((ff, width), BF16),
            pltpu.VMEM((tokens, width), BF16), pltpu.VMEM((tokens, width), BF16),
            pltpu.VMEM((tokens, ff), BF16), pltpu.VMEM((tokens, ff), BF16),
        ],
        12 * tokens * width * ff, tokens * ff,
        where, *xs, *gs, own, other,
    )


def expert_kernel(rows, ne, where_ref, *refs):
    x_ref, c_ref, wi_own, wi_other, wo_own, wo_other, router_ref, mine_ref = refs[:8]
    y_ref, dx_ref, gi_own, gi_other, go_own, go_other, gr_ref = refs[8:15]
    wi_ref, wo_ref, g_ref, act_ref, dh_ref = refs[15:]
    width = x_ref.shape[1]
    ff = wo_ref.shape[0]
    half = ff // 2
    wi_ref[:, :half] = wi_own[...]
    wi_ref[:, half:ff] = wi_other[...]
    wi_ref[:, ff:] = router_ref[...]
    wo_ref[:half, :] = wo_own[...]
    wo_ref[half:, :] = wo_other[...]
    mine = mine_ref[...]
    lanes = lax.broadcasted_iota(jnp.int32, (rows, mine.shape[1]), 1)

    @pl.loop(0, x_ref.shape[0] // rows)
    def _(t):
        r = pl.ds(pl.multiple_of(t * rows, rows), rows)
        hidden = dot(x_ref[r, :], wi_ref[...])
        logits = jnp.where(lanes < ne, hidden[:, ff:], NEG)
        raised = jnp.exp(logits - jnp.max(logits, axis=1, keepdims=True))
        probs = raised / jnp.sum(raised, axis=1, keepdims=True)
        gate = jnp.sum(probs * mine, axis=1, keepdims=True)
        act, slope = gelu_pair(hidden[:, :ff])
        act = act.astype(BF16)
        cot = c_ref[r, :].astype(F32)
        grad = (gate * cot).astype(BF16)
        dh = (dot_nt(grad, wo_ref[...]) * slope).astype(BF16)
        result = dot(act, wo_ref[...])
        d_gate = jnp.sum(cot * result, axis=1, keepdims=True)
        act_ref[r, :] = act
        g_ref[r, :] = grad
        dh_ref[r, :ff] = dh
        dh_ref[r, ff:] = (d_gate * probs * (mine - gate)).astype(BF16)
        y_ref[r, :] = result.astype(BF16)
        dx_ref[r, :] = dot_nt(dh_ref[r, :], wi_ref[...]).astype(BF16)

    go_other[...] = dot_tn(act_ref[:, half:], g_ref[...]).astype(BF16)
    go_own[...] = dot_tn(act_ref[:, :half], g_ref[...]).astype(BF16)
    for j in range(2):
        c = pl.ds(j * (width // 2), width // 2)
        grad = dot_tn(x_ref[:, c], dh_ref[...])
        gi_own[c, :] = grad[:, :half].astype(BF16)
        gi_other[c, :] = grad[:, half:ff].astype(BF16)
        gr_ref[c, :] = grad[:, ff:]


def expert_block(where, x, cot, wi_own, wi_other, wo_own, wo_other, router, mine, rows, ne):
    tokens, width = x.shape
    ff, pad = 2 * wo_own.shape[0], router.shape[1]
    return vmem_call(
        functools.partial(expert_kernel, rows, ne),
        [shape16(tokens, width)] * 2
        + [shape16(*w.shape) for w in (wi_own, wi_other, wo_own, wo_other)]
        + [jax.ShapeDtypeStruct((width, pad), F32)],
        [
            pltpu.VMEM((width, ff + pad), BF16), pltpu.VMEM((ff, width), BF16),
            pltpu.VMEM((tokens, width), BF16),
            pltpu.VMEM((tokens, ff), BF16), pltpu.VMEM((tokens, ff + pad), BF16),
        ],
        12 * tokens * width * ff, tokens * ff,
        where, x, cot, wi_own, wi_other, wo_own, wo_other, router, mine,
    )


def solution(mesh):
    nd, nc, ne = (mesh.shape[a] for a in AXES)
    ndev = nd * nc * ne
    bits_of = lambda n: [1 << b for b in range(n.bit_length() - 1)]
    low_bits, all_bits = bits_of(nc), bits_of(ne)
    high_bits = [b for b in all_bits if b not in low_bits]
    nh = ne // nc


    def send(x, target):
        pairs = []
        for d in range(nd):
            for c in range(nc):
                for e in range(ne):
                    to = target(d, c, e)
                    if to is not None:
                        pairs.append(((d * nc + c) * ne + e, (to[0] * nc + to[1]) * ne + to[2]))
        return lax.ppermute(x, AXES, pairs)

    def swap_exp(x, bit):
        return send(x, lambda d, c, e: (d, c, e ^ bit))

    def swap_dp(x):
        return send(x, lambda d, c, e: (d ^ 1, c, e))

    def reverse(i):
        return int(format(i, "b").zfill(len(low_bits))[::-1], 2)

    def to_seq(x):
        return send(x, lambda d, c, e: (d, reverse(e % nc), e - e % nc + c))

    def from_seq(x):
        return send(x, lambda d, c, e: (d, e % nc, e - e % nc + reverse(c)))

    def to_seq_by(x, *others):
        x = after(swap_exp(x, nc // 2), *others)
        return send(x, lambda d, c, e: (d, reverse((e ^ (nc // 2)) % nc), e - e % nc + c))

    def from_seq_by(x):
        x = send(x, lambda d, c, e: (d, e % nc, (e - e % nc + reverse(c)) ^ (nc // 2)))
        return swap_exp(x, nc // 2)

    def after(x, *others):
        return lax.optimization_barrier((x,) + others)[0]

    def my_bit(bit):
        return (lax.axis_index("exp") // bit) % 2

    def ordered(mine, other, index, axis):
        return jnp.where(
            index == 0, jnp.stack([mine, other], axis), jnp.stack([other, mine], axis)
        )

    def gather_exp(x, bits):
        out = x[None]
        for bit in reversed(bits):
            out = ordered(out, swap_exp(out, bit), my_bit(bit), 1)
            out = out.reshape((-1,) + x.shape)
        return out

    def pieces_exp(x, bits):
        out = [x]
        for bit in reversed(bits):
            out = [v for own in out for v in (own, swap_exp(own, bit))]
        return out

    def scatter_exp_rel(keep, away, bits):
        parts = keep.astype(F32) + swap_exp(away, bits[0]).astype(F32)
        for bit in bits[1:]:
            pairs = parts.reshape((parts.shape[0], -1, 2) + parts.shape[2:])
            away = swap_exp(pairs[:, :, 1].astype(BF16), bit)
            parts = pairs[:, :, 0].astype(F32) + away.astype(F32)
        return parts[:, 0], away

    def split_bit(x, position, count):
        shape = x.shape
        return x.reshape((shape[0] >> (position + 1), 2, 1 << position) + shape[1:])

    def scatter_exp(parts, bits):
        for bit in bits:
            pairs = parts.reshape((-1, 2) + parts.shape[1:])
            mine = my_bit(bit)
            keep = lax.dynamic_index_in_dim(pairs, mine, 1, keepdims=False)
            away = lax.dynamic_index_in_dim(pairs, 1 - mine, 1, keepdims=False)
            parts = keep.astype(F32) + swap_exp(away.astype(BF16), bit).astype(F32)
        return parts[0]

    def trade_exp(parts, bits):
        for position, bit in enumerate(bits):
            pairs = split_bit(parts, position, len(bits))
            mine = my_bit(bit)
            keep = lax.dynamic_index_in_dim(pairs, mine, 1, keepdims=False)
            away = lax.dynamic_index_in_dim(pairs, 1 - mine, 1, keepdims=False)
            parts = ordered(keep, swap_exp(away, bit), mine, 1).reshape(parts.shape)
        return parts

    def gather_ctx(x):
        return lax.all_to_all(
            jnp.broadcast_to(x[None], (nc,) + x.shape), "ctx", 0, 0, tiled=True
        )

    def scatter_ctx(parts):
        parts = lax.all_to_all(parts.astype(BF16), "ctx", 0, 0, tiled=True)
        return jnp.sum(parts.astype(F32), axis=0)

    def scatter_plane(own, other, *others):
        both = (own.astype(F32) + other.astype(F32)).astype(BF16)
        return scatter_ctx(after(both, *others))

    def out_place(d, c, e):
        low, rest = divmod((d * nc + c) * ne + e, ndev // nc)
        return rest // (nc * nh), rest // nh % nc, rest % nh * nc + low

    def out_to(x):
        return send(x, out_place)

    def out_from(x):
        back = {
            out_place(d, c, e): (d, c, e) for d in range(nd) for c in range(nc) for e in range(ne)
        }
        return send(x, lambda d, c, e: back[(d, c, e)])

    def per_device(
        tokens, qkv_weight, out_weight, norm1_gain, norm1_shift, norm2_gain, norm2_shift,
        inner_weight, outer_weight, router_weight, expert_inner, expert_outer,
        segments, routes, priority, cotangent,
    ):
        rows, width = tokens.shape[1:]
        length = segments.shape[1]
        rw = qkv_weight.shape[0]
        ff_rows = outer_weight.shape[0]
        nplane = nd * nc
        e_here = lax.axis_index("exp")
        group = width // nc

        x_low = to_seq(tokens[0])
        capacity = (9 * rows + 8 * ne - 1) // (8 * ne)
        slots = ne * capacity
        route, order = routes[0, :, 0], priority[0, 0]
        same = route[:, None] == route[None, :]
        earlier = order[None, :] < order[:, None]
        slot = jnp.sum(jnp.logical_and(same, earlier).astype(jnp.int32), axis=1)
        place = jnp.where(slot < capacity, route * capacity + slot, -1)

        table_there = (jnp.arange(slots, dtype=jnp.int32)[:, None] == place[None, :]).astype(BF16)
        ints = jnp.concatenate([segments[0], route, place])
        ints = to_seq(ints.reshape(-1, 128)).reshape(-1)
        segs, route, place = ints[:length], ints[length : length + rows], ints[length + rows :]

        def table_of(place):
            return (jnp.arange(slots, dtype=jnp.int32)[:, None] == place[None, :]).astype(BF16)

        table = table_of(place)

        def rows_out(table, v):
            return dot(table, v).astype(BF16).reshape(ne, capacity, width)

        def to_experts(table, v):
            out = jnp.broadcast_to(rows_out(table, v)[None], (nc, ne, capacity, width))
            out = out.reshape(nc * ne, capacity, width)
            return lax.all_to_all(out, ("ctx", "exp"), 0, 0, tiled=True)

        def from_experts(v):
            back = v.reshape(nc * ne, capacity, width)
            back = lax.all_to_all(back, ("ctx", "exp"), 0, 0, tiled=True)
            return dot_tn(jnp.tile(table, (nc, 1)), back.reshape(nc * slots, width)), back

        small = jnp.concatenate(
            [norm1_gain, norm1_shift, norm2_gain, norm2_shift, router_weight.reshape(-1)]
        )
        small = lax.all_to_all(
            jnp.broadcast_to(small[None], (ndev,) + small.shape), AXES, 0, 0, tiled=True
        )
        ff = nplane * ff_rows
        where = jnp.stack([e_here % nc, lax.axis_index("dp")]).astype(jnp.int32)
        qkv_part = jnp.moveaxis(qkv_weight.reshape(rw, 3, nc, group), 2, 0)
        qkv_part = jnp.tile(qkv_part.reshape(nc, rw, 3 * group), (nh, 1, 1))
        inner_part = jnp.moveaxis(inner_weight.reshape(rw, nplane, ne, ff_rows), 2, 0)
        columns = jnp.concatenate([qkv_part, inner_part.reshape(ne, rw, ff)], axis=2)
        columns = lax.all_to_all(columns, "exp", 0, 0, tiled=True).reshape(ne * rw, -1)
        out_part = gather_exp(out_to(out_weight), high_bits).reshape(nh * rw, nc, group)
        out_part = jnp.swapaxes(out_part, 0, 1).reshape(ne * rw, group)
        bundle = jnp.concatenate([columns[:, : 3 * group], out_part], axis=1)
        cot_low = to_seq_by(cotangent[0])
        ei_other = swap_dp(expert_inner[0])
        att_own = gather_ctx(after(bundle, x_low, ei_other))
        ei_own, eo_own = expert_inner[0], expert_outer[0]
        gain1, shift1, gain2, shift2 = (
            small[:, i * rw : (i + 1) * rw].reshape(width).astype(F32) for i in range(4)
        )
        router = small[:, 4 * rw :].reshape(width, ne)

        x = x_low.astype(F32)
        unit1, scale1 = norm_parts(x)
        normed = pieces_exp((unit1 * gain1 + shift1).astype(BF16), low_bits)
        att_other = swap_dp(att_own)
        eo_other = swap_dp(after(eo_own, att_other))
        qkv, attended, keep, away = attention_fwd(where, normed, att_own, att_other, segs)
        e_cot = trade_exp(rows_out(table_there, cotangent[0]), all_bits)
        part = columns[:, 3 * group :].reshape(width // ff, -1, ff)
        part = jnp.concatenate([jnp.swapaxes(part, 0, 1).reshape(-1, width), outer_weight])
        ff_own = gather_ctx(after(part, att_own, e_cot))
        ff_other = swap_dp(ff_own)
        keep = after(keep, ff_own, eo_other)
        residual = x + scatter_exp_rel(keep[None], away[None], low_bits)[0][0]
        e_cot = gather_ctx(after(e_cot, ff_own, keep)).reshape(nc, nh, nc, capacity, width)
        cot_all = pieces_exp(cot_low, all_bits)
        residual = after(residual, *cot_all)
        unit2, scale2 = norm_parts(residual)
        normed2 = (unit2 * gain2 + shift2).astype(BF16)

        cot = cot_low.astype(F32)
        e_cot = jnp.stack([e_cot[:, :, reverse(c)] for c in range(nc)])
        e_cot = jnp.moveaxis(e_cot, 1, 2).reshape(nc * slots, width)
        e_x = to_experts(table, normed2).reshape(nc * slots, width)
        n2_all = pieces_exp(normed2, all_bits)
        keep, away, ff_keep, ff_away = dense_block(where, n2_all, cot_all, ff_own, ff_other, ff)
        ff_away = swap_dp(ff_away)
        both, last = scatter_exp_rel(keep, away, all_bits)
        dense, d_n2_dense = both[0], both[1]

        e_x = after(e_x, keep)
        mine = (jnp.arange(128, dtype=jnp.int32) == e_here).astype(F32)[None, :]
        lanes = jnp.pad(router, ((0, 0), (0, 128 - ne)))
        e_result, d_e_x, gi_own, gi_other, go_own, go_other, d_router = expert_block(
            where, e_x, e_cot, ei_own, ei_other, eo_own, eo_other, lanes, mine,
            nc * slots // 4, ne,
        )
        d_router = d_router[:, :ne]
        gi_other, go_other = swap_dp(gi_other), swap_dp(go_other)

        d_e_x = after(d_e_x, ff_away, last)
        d_e_x, back = from_experts(d_e_x)
        d_n2 = d_n2_dense + d_e_x
        g_e_in = gi_own.astype(F32) + gi_other.astype(F32)
        g_e_out = go_own.astype(F32) + go_other.astype(F32)
        d_gain2 = jnp.sum(d_n2 * unit2, axis=0)
        d_shift2 = jnp.sum(d_n2, axis=0)
        d_residual = cot + norm_back(d_n2, unit2, scale2, gain2)
        d_branch = pieces_exp(d_residual.astype(BF16), low_bits)
        part = scatter_plane(ff_keep, ff_away, back, gi_other, go_other)
        e_result = scatter_ctx(after(e_result, part).reshape(nc, slots, width)).astype(BF16)
        picked = trade_exp(e_result.reshape(ne, capacity, width), all_bits)
        picked = dot_tn(table, picked.reshape(slots, width))
        probs = softmax_rows(dot(normed2, router))
        chosen = (route[:, None] == jnp.arange(ne, dtype=jnp.int32)[None, :]).astype(F32)
        gate = jnp.sum(probs * chosen, axis=1, keepdims=True)
        output = from_seq((residual + dense + gate * picked).astype(BF16))

        d_branch[0] = after(d_branch[0], part)
        keep, away, att_keep, att_away = attention_bwd(
            where, d_branch, normed, att_own, att_other, segs, qkv, attended
        )
        d_normed = scatter_exp_rel(keep[None], away[None], low_bits)[0][0]
        d_gain1 = jnp.sum(d_normed * unit1, axis=0)
        d_shift1 = jnp.sum(d_normed, axis=0)
        d_tokens = d_residual + norm_back(d_normed, unit1, scale1, gain1)
        d_tokens = from_seq(d_tokens.astype(BF16)).astype(F32)

        g_outer = part[width * ff // (nplane * width) :]
        g_inner = part[: width * ff // (nplane * width)].reshape(-1, width // ff, ff)
        g_inner = jnp.swapaxes(g_inner, 0, 1).reshape(ne, rw, ff)
        bundle = scatter_plane(att_keep, swap_dp(att_away), e_result)
        g_out = bundle[:, 3 * group :].reshape(nc, nh * rw, group)
        g_out = jnp.swapaxes(g_out, 0, 1).reshape(nh, rw, width)
        g_out = out_from(scatter_exp(g_out, high_bits).astype(BF16)).astype(F32)
        g_qkv = bundle[:, : 3 * group].reshape(ne, rw, 3 * group)
        columns = jnp.concatenate([g_qkv, g_inner], axis=2).astype(BF16)
        columns = lax.all_to_all(columns, "exp", 0, 0, tiled=True)
        g_inner = columns[:, :, 3 * group :].reshape(ne, rw, nplane, ff_rows)
        g_inner = jnp.transpose(g_inner, (1, 2, 0, 3)).reshape(rw, -1).astype(F32)
        g_qkv = columns[:, :, : 3 * group].reshape(nh, nc, rw, 3, group)
        g_qkv = jnp.sum(g_qkv.astype(F32), axis=0)
        g_qkv = jnp.transpose(g_qkv, (1, 2, 0, 3)).reshape(rw, 3 * width)

        small = jnp.concatenate([jnp.stack([d_gain1, d_shift1, d_gain2, d_shift2], 1), d_router], 1)
        small = after(small.reshape(ndev, -1), bundle)
        small = lax.all_to_all(small, AXES, 0, 0, tiled=True)
        small = jnp.sum(small, axis=0).reshape(rw, 4 + ne)

        return (
            output[None], d_tokens[None], g_qkv, g_out,
            small[:, 0], small[:, 1], small[:, 2], small[:, 3],
            g_inner, g_outer, small[:, 4:], g_e_in[None].astype(F32), g_e_out[None].astype(F32),
        )

    rest = ("dp", "ctx", "exp")
    seq = P(("dp", "exp"), "ctx", None)
    in_specs = (
        seq, P(rest, None), P(rest, None), P(rest), P(rest), P(rest), P(rest),
        P(rest, None), P(rest, None), P(rest, None),
        P("exp", None, ("dp", "ctx")), P("exp", ("dp", "ctx"), None),
        P(("dp", "exp"), None), seq, seq, seq,
    )
    out_specs = (
        seq, seq, P(rest, None), P(rest, None), P(rest), P(rest), P(rest), P(rest),
        P(rest, None), P(rest, None), P(rest, None),
        P("exp", None, ("dp", "ctx")), P("exp", ("dp", "ctx"), None),
    )
    return jax.shard_map(
        per_device, mesh=mesh, in_specs=in_specs, out_specs=out_specs, check_vma=False
    )
```

```python
import functools
import math

import jax
import jax.numpy as jnp
from jax import lax
from jax.experimental import pallas as pl
from jax.experimental.pallas import tpu as pltpu
from jax.sharding import PartitionSpec as P

HEADS = 16
HEAD_DIM = 64
AXES = ("dp", "ctx", "exp")
EPS = 1e-05
NEG = -1e30
GELU_A = 0.7978845608028654
GELU_B = 0.044715
SPREAD = 10
F32 = jnp.float32
BF16 = jnp.bfloat16


def dot(a, b):
    return jnp.dot(a, b, preferred_element_type=F32)


def dot_nt(a, b):
    return lax.dot_general(a, b, (((1,), (1,)), ((), ())), preferred_element_type=F32)


def dot_tn(a, b):
    return lax.dot_general(a, b, (((0,), (0,)), ((), ())), preferred_element_type=F32)


def norm_parts(z):
    average = jnp.mean(z, axis=-1, keepdims=True)
    centred = z - average
    scale = lax.rsqrt(jnp.mean(centred * centred, axis=-1, keepdims=True) + EPS)
    return centred * scale, scale


def norm_back(grad, unit, scale, gain):
    w = grad * gain
    return scale * (
        w
        - jnp.mean(w, axis=-1, keepdims=True)
        - unit * jnp.mean(w * unit, axis=-1, keepdims=True)
    )


def gelu_pair(u):
    square = u * u
    t = jnp.tanh(u * (GELU_A + GELU_A * GELU_B * square))
    half = 0.5 * (1.0 + t)
    return u * half, half + 0.5 * u * (1.0 - t * t) * (GELU_A + 3.0 * GELU_A * GELU_B * square)


def softmax_rows(v):
    raised = jnp.exp(v - jnp.max(v, axis=-1, keepdims=True))
    return raised / jnp.sum(raised, axis=-1, keepdims=True)


def assemble(full_ref, own, other, here):
    half = full_ref.shape[0] // 2
    full_ref[pl.ds(pl.multiple_of(here * half, half), half), :] = own
    full_ref[pl.ds(pl.multiple_of((1 - here) * half, half), half), :] = other


def assemble_attention(n, own_ref, other_ref, w_ref, wo_ref, here):
    planes, rows, width = own_ref.shape
    group = width // n
    small = wo_ref.shape[0] // (2 * planes)
    for ref, d in ((own_ref, here), (other_ref, 1 - here)):
        for c in range(planes):
            at = pl.multiple_of((d * planes + c) * rows, rows)
            w_ref[pl.ds(at, rows), :] = ref[c, :, : 3 * group]
            at = pl.multiple_of((d * planes + c) * small, small)
            for g in range(n):
                wo_ref[pl.ds(at, small), g * group : (g + 1) * group] = ref[
                    c, g * small : (g + 1) * small, 3 * group :
                ]


def attention_fwd_kernel(n, where_ref, *refs):
    xs, refs = refs[:n], refs[n:]
    own_ref, other_ref, segrow_ref, segcol_ref = refs[:4]
    qkv_ref, att_ref, keep_ref, away_ref, w_ref, wo_ref = refs[4:]
    block = xs[0].shape[0]
    group = att_ref.shape[1]
    pair = 2 * HEAD_DIM
    low, here = where_ref[0], where_ref[1]
    scale = 1.0 / math.sqrt(HEAD_DIM)
    assemble_attention(n, own_ref, other_ref, w_ref, wo_ref, here)

    def natural(i):
        return pl.ds(pl.multiple_of((low ^ i) * block, block), block)

    for i in range(n):
        qkv_ref[natural(i), :] = dot(xs[i][...], w_ref[...]).astype(BF16)

    first = lax.broadcasted_iota(jnp.int32, (block, pair), 1) < HEAD_DIM

    @pl.loop(0, group // pair)
    def _(p):
        lanes = [pl.ds(pl.multiple_of(j * group + p * pair, pair), pair) for j in range(3)]
        for i in range(n):
            ext = (i + 1) * block
            rows = pl.ds(i * block, block)
            q = qkv_ref[rows, lanes[0]] * jnp.asarray(scale, BF16)
            k = qkv_ref[pl.ds(0, ext), lanes[1]]
            v = qkv_ref[pl.ds(0, ext), lanes[2]]
            qpos = lax.broadcasted_iota(jnp.int32, (block, ext), 0) + i * block
            kpos = lax.broadcasted_iota(jnp.int32, (block, ext), 1)
            visible = jnp.logical_and(
                kpos <= qpos, segcol_ref[rows, :] == segrow_ref[:, pl.ds(0, ext)]
            )
            outs = []
            for half in range(2):
                mine = first if half == 0 else jnp.logical_not(first)
                s = jnp.where(visible, dot_nt(jnp.where(mine, q, jnp.zeros_like(q)), k), NEG)
                e = jnp.exp(s - jnp.max(s, axis=1, keepdims=True))
                outs.append(dot(e.astype(BF16), v) / jnp.sum(e, axis=1, keepdims=True))
            att_ref[rows, lanes[0]] = jnp.where(first, outs[0], outs[1]).astype(BF16)

    for i in range(n):
        part = dot(att_ref[natural(i), :], wo_ref[...]).astype(BF16)
        (away_ref if i % 2 else keep_ref)[i // 2] = part


def attention_bwd_kernel(n, where_ref, *refs):
    ds_in, xs, refs = refs[:n], refs[n : 2 * n], refs[2 * n :]
    own_ref, other_ref, segrow_ref, segcol_ref, qkv_ref, att_ref = refs[:6]
    keep_ref, away_ref, gown_ref, gother_ref = refs[6:10]
    w_ref, wo_ref, x_ref, db_ref, do_ref, dqkv_ref, dk_acc, dv_acc = refs[10:]
    block = xs[0].shape[0]
    length, group = att_ref.shape
    width = x_ref.shape[1]
    planes, wrows = own_ref.shape[:2]
    small = group // (2 * planes)
    pair = 2 * HEAD_DIM
    low, here = where_ref[0], where_ref[1]
    scale = 1.0 / math.sqrt(HEAD_DIM)
    assemble_attention(n, own_ref, other_ref, w_ref, wo_ref, here)

    def natural(i):
        return pl.ds(pl.multiple_of((low ^ i) * block, block), block)

    for i in range(n):
        x_ref[natural(i), :] = xs[i][...]
        db_ref[natural(i), :] = ds_in[i][...]
        do_ref[natural(i), :] = dot_nt(ds_in[i][...], wo_ref[...]).astype(BF16)

    first = lax.broadcasted_iota(jnp.int32, (block, pair), 1) < HEAD_DIM

    @pl.loop(0, group // pair)
    def _(p):
        lanes = [pl.ds(pl.multiple_of(j * group + p * pair, pair), pair) for j in range(3)]
        dk_acc[...] = jnp.zeros_like(dk_acc)
        dv_acc[...] = jnp.zeros_like(dv_acc)
        for i in range(n):
            ext = (i + 1) * block
            rows = pl.ds(i * block, block)
            keys = pl.ds(0, ext)
            q = qkv_ref[rows, lanes[0]] * jnp.asarray(scale, BF16)
            do = do_ref[rows, lanes[0]]
            k = qkv_ref[keys, lanes[1]]
            v = qkv_ref[keys, lanes[2]]
            qpos = lax.broadcasted_iota(jnp.int32, (ext, block), 1) + i * block
            kpos = lax.broadcasted_iota(jnp.int32, (ext, block), 0)
            visible = jnp.logical_and(kpos <= qpos, segcol_ref[keys, :] == segrow_ref[:, rows])
            dq = []
            for half in range(2):
                mine = first if half == 0 else jnp.logical_not(first)
                qh = jnp.where(mine, q, jnp.zeros_like(q))
                doh = jnp.where(mine, do, jnp.zeros_like(do))
                s = jnp.where(visible, dot_nt(k, qh), NEG)
                e = jnp.exp(s - jnp.max(s, axis=0, keepdims=True))
                e = e * (1.0 / jnp.sum(e, axis=0, keepdims=True))
                dp = dot_nt(v, doh)
                delta = jnp.sum(e * dp, axis=0, keepdims=True)
                ds = (e * (dp - delta)).astype(BF16)
                dv_acc[keys, :] += dot(e.astype(BF16), doh)
                dk_acc[keys, :] += dot(ds, qh)
                dq.append(dot_tn(ds, k))
            dqkv_ref[rows, lanes[0]] = (jnp.where(first, dq[0], dq[1]) * scale).astype(BF16)
        dqkv_ref[:, lanes[1]] = dk_acc[...].astype(BF16)
        dqkv_ref[:, lanes[2]] = dv_acc[...].astype(BF16)

    for i in range(n):
        part = dot_nt(dqkv_ref[natural(i), :], w_ref[...]).astype(BF16)
        (away_ref if i % 2 else keep_ref)[i // 2] = part
    wo_ref[...] = dot_tn(att_ref[...], db_ref[...]).astype(BF16)
    for ref, d in ((gown_ref, here), (gother_ref, 1 - here)):
        at = pl.ds(pl.multiple_of(d * (width // 2), width // 2), width // 2)
        grad = dot_tn(x_ref[:, at], dqkv_ref[...]).astype(BF16)
        for c in range(planes):
            ref[c, :, : 3 * group] = grad[c * wrows : (c + 1) * wrows]
            at = pl.multiple_of((d * planes + c) * small, small)
            for g in range(n):
                ref[c, g * small : (g + 1) * small, 3 * group :] = wo_ref[
                    pl.ds(at, small), g * group : (g + 1) * group
                ]


def vmem_call(kernel, out_shape, scratch, flops, transcendentals, where, *args):
    bytes_of = lambda a: math.prod(a.shape) * a.dtype.itemsize
    vmem = pl.BlockSpec(memory_space=pltpu.VMEM)
    return pl.pallas_call(
        kernel,
        in_specs=[pl.BlockSpec(memory_space=pltpu.SMEM)] + [vmem] * len(args),
        out_specs=[vmem] * len(out_shape),
        out_shape=out_shape,
        scratch_shapes=scratch,
        compiler_params=pltpu.CompilerParams(vmem_limit_bytes=60 * 1024 * 1024),
        cost_estimate=pl.CostEstimate(
            flops=SPREAD * flops,
            bytes_accessed=sum(map(bytes_of, args)) + sum(map(bytes_of, out_shape)),
            transcendentals=transcendentals,
        ),
    )(where, *args)


def shape16(*dims):
    return jax.ShapeDtypeStruct(dims, BF16)


def attention_fwd(where, xs, own, other, segs):
    n, (block, width) = len(xs), xs[0].shape
    length, group = n * block, width // n
    return vmem_call(
        functools.partial(attention_fwd_kernel, n),
        [
            shape16(length, 3 * group), shape16(length, group),
            shape16(n // 2, block, width), shape16(n // 2, block, width),
        ],
        [pltpu.VMEM((width, 3 * group), BF16), pltpu.VMEM((group, width), BF16)],
        8 * length * width * group + 8 * length * length * group,
        length * length * group // HEAD_DIM // 2,
        where, *xs, own, other, segs[None, :], segs[:, None],
    )


def attention_bwd(where, d_branch, xs, own, other, segs, qkv, att):
    n, (block, width) = len(xs), xs[0].shape
    length, group = n * block, width // n
    return vmem_call(
        functools.partial(attention_bwd_kernel, n),
        [
            shape16(n // 2, block, width), shape16(n // 2, block, width),
            shape16(*own.shape), shape16(*own.shape),
        ],
        [
            pltpu.VMEM((width, 3 * group), BF16), pltpu.VMEM((group, width), BF16),
            pltpu.VMEM((length, width), BF16), pltpu.VMEM((length, width), BF16),
            pltpu.VMEM((length, group), BF16), pltpu.VMEM((length, 3 * group), BF16),
            pltpu.VMEM((length, 2 * HEAD_DIM), F32), pltpu.VMEM((length, 2 * HEAD_DIM), F32),
        ],
        16 * length * width * group + 20 * length * length * group,
        length * length * group // HEAD_DIM // 2,
        where, *d_branch, *xs, own, other, segs[None, :], segs[:, None], qkv, att,
    )


def dense_kernel(n, ff, where_ref, *refs):
    xs, gs, refs = refs[:n], refs[n : 2 * n], refs[2 * n :]
    own_ref, other_ref, keep_ref, away_ref, gown_ref, gother_ref = refs[:6]
    wi_ref, wo_ref, x_ref, g_ref, act_ref, dh_ref = refs[6:]
    rows, width = xs[0].shape
    planes = own_ref.shape[0]
    here = where_ref[1]
    inner, outer = width // (2 * planes), ff // (2 * planes)
    for ref, d in ((own_ref, here), (other_ref, 1 - here)):
        for c in range(planes):
            at = pl.multiple_of((d * planes + c) * inner, inner)
            for g in range(width // ff):
                wi_ref[pl.ds(at + g * (inner * ff // width), inner * ff // width), :] = ref[
                    c, : inner * ff // width, g * ff : (g + 1) * ff
                ]
            at = pl.multiple_of((d * planes + c) * outer, outer)
            wo_ref[pl.ds(at, outer), :] = ref[c, inner * ff // width :, :]
    for i in range(n):
        x_ref[pl.ds(i * rows, rows), :] = xs[i][...]
        g_ref[pl.ds(i * rows, rows), :] = gs[i][...]

    @pl.loop(0, n // 2)
    def _(t):
        for odd, out_ref in ((0, keep_ref), (1, away_ref)):
            r = pl.ds(pl.multiple_of((2 * t + odd) * rows, rows), rows)
            act, slope = gelu_pair(dot(x_ref[r, :], wi_ref[...]))
            act = act.astype(BF16)
            dh = (dot_nt(g_ref[r, :], wo_ref[...]) * slope).astype(BF16)
            act_ref[r, :] = act
            dh_ref[r, :] = dh
            out_ref[0, t] = dot(act, wo_ref[...]).astype(BF16)
            out_ref[1, t] = dot_nt(dh, wi_ref[...]).astype(BF16)

    small = inner * ff // width
    for ref, d in ((gother_ref, 1 - here), (gown_ref, here)):
        c = pl.ds(pl.multiple_of(d * (ff // 2), ff // 2), ff // 2)
        grad = dot_tn(act_ref[:, c], g_ref[...]).astype(BF16)
        ref[:, small:, :] = grad.reshape(planes, outer, width)
        c = pl.ds(pl.multiple_of(d * (width // 2), width // 2), width // 2)
        grad = dot_tn(x_ref[:, c], dh_ref[...]).astype(BF16).reshape(planes, inner, ff)
        for g in range(width // ff):
            ref[:, :small, g * ff : (g + 1) * ff] = grad[:, g * small : (g + 1) * small]


def dense_block(where, xs, gs, own, other, ff):
    n, (rows, width) = len(xs), xs[0].shape
    tokens = n * rows
    both = shape16(2, n // 2, rows, width)
    return vmem_call(
        functools.partial(dense_kernel, n, ff),
        [both, both, shape16(*own.shape), shape16(*own.shape)],
        [
            pltpu.VMEM((width, ff), BF16), pltpu.VMEM((ff, width), BF16),
            pltpu.VMEM((tokens, width), BF16), pltpu.VMEM((tokens, width), BF16),
            pltpu.VMEM((tokens, ff), BF16), pltpu.VMEM((tokens, ff), BF16),
        ],
        12 * tokens * width * ff, tokens * ff,
        where, *xs, *gs, own, other,
    )


def expert_kernel(rows, ne, where_ref, *refs):
    x_ref, c_ref, wi_own, wi_other, wo_own, wo_other, router_ref, mine_ref = refs[:8]
    y_ref, dx_ref, gi_own, gi_other, go_own, go_other, gr_ref = refs[8:15]
    wi_ref, wo_ref, g_ref, act_ref, dh_ref = refs[15:]
    width = x_ref.shape[1]
    ff = wo_ref.shape[0]
    half = ff // 2
    wi_ref[:, :half] = wi_own[...]
    wi_ref[:, half:ff] = wi_other[...]
    wi_ref[:, ff:] = router_ref[...]
    wo_ref[:half, :] = wo_own[...]
    wo_ref[half:, :] = wo_other[...]
    mine = mine_ref[...]
    lanes = lax.broadcasted_iota(jnp.int32, (rows, mine.shape[1]), 1)

    @pl.loop(0, x_ref.shape[0] // rows)
    def _(t):
        r = pl.ds(pl.multiple_of(t * rows, rows), rows)
        hidden = dot(x_ref[r, :], wi_ref[...])
        logits = jnp.where(lanes < ne, hidden[:, ff:], NEG)
        raised = jnp.exp(logits - jnp.max(logits, axis=1, keepdims=True))
        probs = raised / jnp.sum(raised, axis=1, keepdims=True)
        gate = jnp.sum(probs * mine, axis=1, keepdims=True)
        act, slope = gelu_pair(hidden[:, :ff])
        act = act.astype(BF16)
        cot = c_ref[r, :].astype(F32)
        grad = (gate * cot).astype(BF16)
        dh = (dot_nt(grad, wo_ref[...]) * slope).astype(BF16)
        result = dot(act, wo_ref[...])
        d_gate = jnp.sum(cot * result, axis=1, keepdims=True)
        act_ref[r, :] = act
        g_ref[r, :] = grad
        dh_ref[r, :ff] = dh
        dh_ref[r, ff:] = (d_gate * probs * (mine - gate)).astype(BF16)
        y_ref[r, :] = result.astype(BF16)
        dx_ref[r, :] = dot_nt(dh_ref[r, :], wi_ref[...]).astype(BF16)

    go_other[...] = dot_tn(act_ref[:, half:], g_ref[...]).astype(BF16)
    go_own[...] = dot_tn(act_ref[:, :half], g_ref[...]).astype(BF16)
    for j in range(2):
        c = pl.ds(j * (width // 2), width // 2)
        grad = dot_tn(x_ref[:, c], dh_ref[...])
        gi_own[c, :] = grad[:, :half].astype(BF16)
        gi_other[c, :] = grad[:, half:ff].astype(BF16)
        gr_ref[c, :] = grad[:, ff:]


def expert_block(where, x, cot, wi_own, wi_other, wo_own, wo_other, router, mine, rows, ne):
    tokens, width = x.shape
    ff, pad = 2 * wo_own.shape[0], router.shape[1]
    return vmem_call(
        functools.partial(expert_kernel, rows, ne),
        [shape16(tokens, width)] * 2
        + [shape16(*w.shape) for w in (wi_own, wi_other, wo_own, wo_other)]
        + [jax.ShapeDtypeStruct((width, pad), F32)],
        [
            pltpu.VMEM((width, ff + pad), BF16), pltpu.VMEM((ff, width), BF16),
            pltpu.VMEM((tokens, width), BF16),
            pltpu.VMEM((tokens, ff), BF16), pltpu.VMEM((tokens, ff + pad), BF16),
        ],
        12 * tokens * width * ff, tokens * ff,
        where, x, cot, wi_own, wi_other, wo_own, wo_other, router, mine,
    )


def solution(mesh):
    nd, nc, ne = (mesh.shape[a] for a in AXES)
    ndev = nd * nc * ne
    bits_of = lambda n: [1 << b for b in range(n.bit_length() - 1)]
    low_bits, all_bits = bits_of(nc), bits_of(ne)
    high_bits = [b for b in all_bits if b not in low_bits]
    nh = ne // nc


    def send(x, target):
        pairs = []
        for d in range(nd):
            for c in range(nc):
                for e in range(ne):
                    to = target(d, c, e)
                    if to is not None:
                        pairs.append(((d * nc + c) * ne + e, (to[0] * nc + to[1]) * ne + to[2]))
        return lax.ppermute(x, AXES, pairs)

    def swap_exp(x, bit):
        return send(x, lambda d, c, e: (d, c, e ^ bit))

    def swap_dp(x):
        return send(x, lambda d, c, e: (d ^ 1, c, e))

    def reverse(i):
        return int(format(i, "b").zfill(len(low_bits))[::-1], 2)

    def to_seq(x):
        return send(x, lambda d, c, e: (d, reverse(e % nc), e - e % nc + c))

    def from_seq(x):
        return send(x, lambda d, c, e: (d, e % nc, e - e % nc + reverse(c)))

    def to_seq_by(x, *others):
        x = after(swap_exp(x, nc // 2), *others)
        return send(x, lambda d, c, e: (d, reverse((e ^ (nc // 2)) % nc), e - e % nc + c))

    def from_seq_by(x):
        x = send(x, lambda d, c, e: (d, e % nc, (e - e % nc + reverse(c)) ^ (nc // 2)))
        return swap_exp(x, nc // 2)

    def after(x, *others):
        return lax.optimization_barrier((x,) + others)[0]

    def my_bit(bit):
        return (lax.axis_index("exp") // bit) % 2

    def ordered(mine, other, index, axis):
        return jnp.where(
            index == 0, jnp.stack([mine, other], axis), jnp.stack([other, mine], axis)
        )

    def gather_exp(x, bits):
        out = x[None]
        for bit in reversed(bits):
            out = ordered(out, swap_exp(out, bit), my_bit(bit), 1)
            out = out.reshape((-1,) + x.shape)
        return out

    def pieces_exp(x, bits):
        out = [x]
        for bit in reversed(bits):
            out = [v for own in out for v in (own, swap_exp(own, bit))]
        return out

    def scatter_exp_rel(keep, away, bits):
        parts = keep.astype(F32) + swap_exp(away, bits[0]).astype(F32)
        for bit in bits[1:]:
            pairs = parts.reshape((parts.shape[0], -1, 2) + parts.shape[2:])
            away = swap_exp(pairs[:, :, 1].astype(BF16), bit)
            parts = pairs[:, :, 0].astype(F32) + away.astype(F32)
        return parts[:, 0], away

    def split_bit(x, position, count):
        shape = x.shape
        return x.reshape((shape[0] >> (position + 1), 2, 1 << position) + shape[1:])

    def scatter_exp(parts, bits):
        for bit in bits:
            pairs = parts.reshape((-1, 2) + parts.shape[1:])
            mine = my_bit(bit)
            keep = lax.dynamic_index_in_dim(pairs, mine, 1, keepdims=False)
            away = lax.dynamic_index_in_dim(pairs, 1 - mine, 1, keepdims=False)
            parts = keep.astype(F32) + swap_exp(away.astype(BF16), bit).astype(F32)
        return parts[0]

    def trade_exp(parts, bits):
        for position, bit in enumerate(bits):
            pairs = split_bit(parts, position, len(bits))
            mine = my_bit(bit)
            keep = lax.dynamic_index_in_dim(pairs, mine, 1, keepdims=False)
            away = lax.dynamic_index_in_dim(pairs, 1 - mine, 1, keepdims=False)
            parts = ordered(keep, swap_exp(away, bit), mine, 1).reshape(parts.shape)
        return parts

    def gather_ctx(x):
        return lax.all_to_all(
            jnp.broadcast_to(x[None], (nc,) + x.shape), "ctx", 0, 0, tiled=True
        )

    def scatter_ctx(parts):
        parts = lax.all_to_all(parts.astype(BF16), "ctx", 0, 0, tiled=True)
        return jnp.sum(parts.astype(F32), axis=0)

    def scatter_plane(own, other, *others):
        both = (own.astype(F32) + other.astype(F32)).astype(BF16)
        return scatter_ctx(after(both, *others))

    def out_place(d, c, e):
        low, rest = divmod((d * nc + c) * ne + e, ndev // nc)
        return rest // (nc * nh), rest // nh % nc, rest % nh * nc + low

    def out_to(x):
        return send(x, out_place)

    def out_from(x):
        back = {
            out_place(d, c, e): (d, c, e) for d in range(nd) for c in range(nc) for e in range(ne)
        }
        return send(x, lambda d, c, e: back[(d, c, e)])

    def per_device(
        tokens, qkv_weight, out_weight, norm1_gain, norm1_shift, norm2_gain, norm2_shift,
        inner_weight, outer_weight, router_weight, expert_inner, expert_outer,
        segments, routes, priority, cotangent,
    ):
        rows, width = tokens.shape[1:]
        length = segments.shape[1]
        rw = qkv_weight.shape[0]
        ff_rows = outer_weight.shape[0]
        nplane = nd * nc
        e_here = lax.axis_index("exp")
        group = width // nc

        x_low = to_seq(tokens[0])
        capacity = (9 * rows + 8 * ne - 1) // (8 * ne)
        slots = ne * capacity
        route, order = routes[0, :, 0], priority[0, 0]
        same = route[:, None] == route[None, :]
        earlier = order[None, :] < order[:, None]
        slot = jnp.sum(jnp.logical_and(same, earlier).astype(jnp.int32), axis=1)
        place = jnp.where(slot < capacity, route * capacity + slot, -1)

        table_there = (jnp.arange(slots, dtype=jnp.int32)[:, None] == place[None, :]).astype(BF16)
        ints = jnp.concatenate([segments[0], route, place])
        ints = to_seq(ints.reshape(-1, 128)).reshape(-1)
        segs, route, place = ints[:length], ints[length : length + rows], ints[length + rows :]

        def table_of(place):
            return (jnp.arange(slots, dtype=jnp.int32)[:, None] == place[None, :]).astype(BF16)

        table = table_of(place)

        def rows_out(table, v):
            return dot(table, v).astype(BF16).reshape(ne, capacity, width)

        def to_experts(table, v):
            out = jnp.broadcast_to(rows_out(table, v)[None], (nc, ne, capacity, width))
            out = out.reshape(nc * ne, capacity, width)
            return lax.all_to_all(out, ("ctx", "exp"), 0, 0, tiled=True)

        def from_experts(v):
            back = v.reshape(nc * ne, capacity, width)
            back = lax.all_to_all(back, ("ctx", "exp"), 0, 0, tiled=True)
            return dot_tn(jnp.tile(table, (nc, 1)), back.reshape(nc * slots, width)), back

        small = jnp.concatenate(
            [norm1_gain, norm1_shift, norm2_gain, norm2_shift, router_weight.reshape(-1)]
        )
        small = lax.all_to_all(
            jnp.broadcast_to(small[None], (ndev,) + small.shape), AXES, 0, 0, tiled=True
        )
        ff = nplane * ff_rows
        where = jnp.stack([e_here % nc, lax.axis_index("dp")]).astype(jnp.int32)
        qkv_part = jnp.moveaxis(qkv_weight.reshape(rw, 3, nc, group), 2, 0)
        qkv_part = jnp.tile(qkv_part.reshape(nc, rw, 3 * group), (nh, 1, 1))
        inner_part = jnp.moveaxis(inner_weight.reshape(rw, nplane, ne, ff_rows), 2, 0)
        columns = jnp.concatenate([qkv_part, inner_part.reshape(ne, rw, ff)], axis=2)
        columns = lax.all_to_all(columns, "exp", 0, 0, tiled=True).reshape(ne * rw, -1)
        out_part = gather_exp(out_to(out_weight), high_bits).reshape(nh * rw, nc, group)
        out_part = jnp.swapaxes(out_part, 0, 1).reshape(ne * rw, group)
        bundle = jnp.concatenate([columns[:, : 3 * group], out_part], axis=1)
        cot_low = to_seq_by(cotangent[0])
        ei_other = swap_dp(expert_inner[0])
        att_own = gather_ctx(after(bundle, x_low, ei_other))
        ei_own, eo_own = expert_inner[0], expert_outer[0]
        gain1, shift1, gain2, shift2 = (
            small[:, i * rw : (i + 1) * rw].reshape(width).astype(F32) for i in range(4)
        )
        router = small[:, 4 * rw :].reshape(width, ne)

        x = x_low.astype(F32)
        unit1, scale1 = norm_parts(x)
        normed = pieces_exp((unit1 * gain1 + shift1).astype(BF16), low_bits)
        att_other = swap_dp(att_own)
        eo_other = swap_dp(after(eo_own, att_other))
        qkv, attended, keep, away = attention_fwd(where, normed, att_own, att_other, segs)
        e_cot = trade_exp(rows_out(table_there, cotangent[0]), all_bits)
        part = columns[:, 3 * group :].reshape(width // ff, -1, ff)
        part = jnp.concatenate([jnp.swapaxes(part, 0, 1).reshape(-1, width), outer_weight])
        ff_own = gather_ctx(after(part, att_own))
        ff_other = swap_dp(ff_own)
        keep = after(keep, ff_own, eo_other)
        residual = x + scatter_exp_rel(keep[None], away[None], low_bits)[0][0]
        e_cot = gather_ctx(after(e_cot, ff_own, keep)).reshape(nc, nh, nc, capacity, width)
        cot_all = pieces_exp(cot_low, all_bits)
        residual = after(residual, *cot_all)
        unit2, scale2 = norm_parts(residual)
        normed2 = (unit2 * gain2 + shift2).astype(BF16)

        cot = cot_low.astype(F32)
        e_cot = jnp.stack([e_cot[:, :, reverse(c)] for c in range(nc)])
        e_cot = jnp.moveaxis(e_cot, 1, 2).reshape(nc * slots, width)
        e_x = to_experts(table, normed2).reshape(nc * slots, width)
        n2_all = pieces_exp(normed2, all_bits)
        keep, away, ff_keep, ff_away = dense_block(where, n2_all, cot_all, ff_own, ff_other, ff)
        ff_away = swap_dp(ff_away)
        both, last = scatter_exp_rel(keep, away, all_bits)
        dense, d_n2_dense = both[0], both[1]

        e_x = after(e_x, keep)
        mine = (jnp.arange(128, dtype=jnp.int32) == e_here).astype(F32)[None, :]
        lanes = jnp.pad(router, ((0, 0), (0, 128 - ne)))
        e_result, d_e_x, gi_own, gi_other, go_own, go_other, d_router = expert_block(
            where, e_x, e_cot, ei_own, ei_other, eo_own, eo_other, lanes, mine,
            nc * slots // 4, ne,
        )
        d_router = d_router[:, :ne]
        gi_other, go_other = swap_dp(gi_other), swap_dp(go_other)

        d_e_x = after(d_e_x, ff_away, last)
        d_e_x, back = from_experts(d_e_x)
        d_n2 = d_n2_dense + d_e_x
        g_e_in = gi_own.astype(F32) + gi_other.astype(F32)
        g_e_out = go_own.astype(F32) + go_other.astype(F32)
        d_gain2 = jnp.sum(d_n2 * unit2, axis=0)
        d_shift2 = jnp.sum(d_n2, axis=0)
        d_residual = cot + norm_back(d_n2, unit2, scale2, gain2)
        d_branch = pieces_exp(d_residual.astype(BF16), low_bits)
        part = scatter_plane(ff_keep, ff_away, back, gi_other, go_other)
        e_result = scatter_ctx(after(e_result, part).reshape(nc, slots, width)).astype(BF16)
        picked = trade_exp(e_result.reshape(ne, capacity, width), all_bits)
        picked = dot_tn(table, picked.reshape(slots, width))
        probs = softmax_rows(dot(normed2, router))
        chosen = (route[:, None] == jnp.arange(ne, dtype=jnp.int32)[None, :]).astype(F32)
        gate = jnp.sum(probs * chosen, axis=1, keepdims=True)
        output = from_seq((residual + dense + gate * picked).astype(BF16))

        d_branch[0] = after(d_branch[0], part)
        keep, away, att_keep, att_away = attention_bwd(
            where, d_branch, normed, att_own, att_other, segs, qkv, attended
        )
        d_normed = scatter_exp_rel(keep[None], away[None], low_bits)[0][0]
        d_gain1 = jnp.sum(d_normed * unit1, axis=0)
        d_shift1 = jnp.sum(d_normed, axis=0)
        d_tokens = d_residual + norm_back(d_normed, unit1, scale1, gain1)
        d_tokens = from_seq(d_tokens.astype(BF16)).astype(F32)

        g_outer = part[width * ff // (nplane * width) :]
        g_inner = part[: width * ff // (nplane * width)].reshape(-1, width // ff, ff)
        g_inner = jnp.swapaxes(g_inner, 0, 1).reshape(ne, rw, ff)
        bundle = scatter_plane(att_keep, swap_dp(att_away), e_result)
        g_out = bundle[:, 3 * group :].reshape(nc, nh * rw, group)
        g_out = jnp.swapaxes(g_out, 0, 1).reshape(nh, rw, width)
        g_out = out_from(scatter_exp(g_out, high_bits).astype(BF16)).astype(F32)
        g_qkv = bundle[:, : 3 * group].reshape(ne, rw, 3 * group)
        columns = jnp.concatenate([g_qkv, g_inner], axis=2).astype(BF16)
        columns = lax.all_to_all(columns, "exp", 0, 0, tiled=True)
        g_inner = columns[:, :, 3 * group :].reshape(ne, rw, nplane, ff_rows)
        g_inner = jnp.transpose(g_inner, (1, 2, 0, 3)).reshape(rw, -1).astype(F32)
        g_qkv = columns[:, :, : 3 * group].reshape(nh, nc, rw, 3, group)
        g_qkv = jnp.sum(g_qkv.astype(F32), axis=0)
        g_qkv = jnp.transpose(g_qkv, (1, 2, 0, 3)).reshape(rw, 3 * width)

        small = jnp.concatenate([jnp.stack([d_gain1, d_shift1, d_gain2, d_shift2], 1), d_router], 1)
        small = after(small.reshape(ndev, -1), bundle)
        small = lax.all_to_all(small, AXES, 0, 0, tiled=True)
        small = jnp.sum(small, axis=0).reshape(rw, 4 + ne)

        return (
            output[None], d_tokens[None], g_qkv, g_out,
            small[:, 0], small[:, 1], small[:, 2], small[:, 3],
            g_inner, g_outer, small[:, 4:], g_e_in[None].astype(F32), g_e_out[None].astype(F32),
        )

    rest = ("dp", "ctx", "exp")
    seq = P(("dp", "exp"), "ctx", None)
    in_specs = (
        seq, P(rest, None), P(rest, None), P(rest), P(rest), P(rest), P(rest),
        P(rest, None), P(rest, None), P(rest, None),
        P("exp", None, ("dp", "ctx")), P("exp", ("dp", "ctx"), None),
        P(("dp", "exp"), None), seq, seq, seq,
    )
    out_specs = (
        seq, seq, P(rest, None), P(rest, None), P(rest), P(rest), P(rest), P(rest),
        P(rest, None), P(rest, None), P(rest, None),
        P("exp", None, ("dp", "ctx")), P("exp", ("dp", "ctx"), None),
    )
    return jax.shard_map(
        per_device, mesh=mesh, in_specs=in_specs, out_specs=out_specs, check_vma=False
    )
```
